256 devices in a mesh: dp: 16 (over x_hi, y, core), tensor: 16 (over x_lo, z).
Axes of the slice: x: 4 (x_hi: 2, x_lo: 2; x = x_hi * 2 + x_lo), y: 4, z: 8, core: 2. Of those that a mesh axis runs over, the one named last changes fastest.
Arguments:
- stored_layer_input: bfloat16 [8192, 4096], P('dp', 'tensor'), may hold values from -6 to 6
- saved_up_output: bfloat16 [8192, 14336], P('dp', 'tensor'), may hold values from -6 to 6
- hidden_gradient: bfloat16 [8192, 14336], P('dp', 'tensor'), may hold values from -6 to 6
- frozen_gate_weight: bfloat16 [4096, 14336], P(None, 'tensor'), may hold values from -1 to 1, as said below
- lowrank_down: bfloat16 [4096, 64], replicated, may hold values from -0.09375 to 0.09375
- lowrank_up: bfloat16 [64, 14336], P(None, 'tensor'), may hold values from -0.75 to 0.75
- magnitude: float32 [14336], P('tensor'), may hold values from 0.5 to 4
Outputs:
- layer_input_gradient: bfloat16 [8192, 4096], P('dp', 'tensor')
- up_output_gradient: bfloat16 [8192, 14336], P('dp', 'tensor')
- lowrank_down_gradient: float32 [4096, 64], P('tensor')
- lowrank_up_gradient: float32 [64, 14336], P(None, 'tensor')
- magnitude_gradient: float32 [14336], P('tensor')
The draws below stay inside these ranges and needn't reach their ends.
Inputs may be any that keep to these rules, and one draw needn't show every extreme that they name: `frozen_gate_weight`: frozen base weights.
All inputs are finite; a program needn't handle non-finite values.
Results may differ from the reference program's by a relative error of at most 0.007.
Values may be sent and summed in bfloat16 or wider, within the bound.
No kernel may reach another device: no remote copies, remote signals or barrier semaphores. Data moves between devices by JAX's collectives and lax.ppermute only.
A program may use at most 128 MiB of HBM per device.

```python
import math
import jax
import jax.numpy as jnp
from jax import lax

MODEL_WIDTH = 4096
HIDDEN_UNITS = 14336
ADAPTER_RANK = 64
TOKENS = 8192


def draw_frozen_gate_weight(key, part):
    key = jax.random.fold_in(key, 11)
    key_one, key_two, key_three = jax.random.split(key, 3)
    entries = jax.random.normal(key_one, (MODEL_WIDTH, HIDDEN_UNITS), jnp.float32)
    row_scale = jnp.exp(jax.random.uniform(key_two, (MODEL_WIDTH, 1), jnp.float32, 0.0, math.log(10.0)))
    ramp = jnp.exp(math.log(3.0) * jnp.arange(HIDDEN_UNITS, dtype=jnp.float32) / HIDDEN_UNITS)
    col_scale = ramp * jnp.exp(jax.random.uniform(key_three, (HIDDEN_UNITS,), jnp.float32, 0.0, math.log(4.0)))
    values = entries * row_scale * col_scale * (1.0 / (20.6 * math.sqrt(MODEL_WIDTH)))
    return jnp.clip(values, -1.0, 1.0).astype(jnp.bfloat16)


def steps_of(stream_key, extent, cuts, low, high):
    factor_of, own = 1.0, jax.random.fold_in(stream_key, 6)
    for axis_at, shards_of in cuts:
        heights = jnp.exp(jax.random.uniform(jax.random.fold_in(own, axis_at), (shards_of,), jnp.float32, low / len(cuts), high / len(cuts)))
        factor_of = factor_of * jnp.repeat(heights, extent[axis_at] // shards_of).reshape([-1 if axis == axis_at else 1 for axis in range(len(extent))])
    return factor_of


def noise(key, dims, scale, reach, cuts=(), kind=jnp.bfloat16):
    level = steps_of(key, dims, cuts, -0.22, 0.18) if cuts else 1.0
    array = jax.random.normal(key, dims, jnp.float32) * scale * level
    return jnp.minimum(jnp.maximum(array, -reach), reach).astype(kind)


def setup_inputs(seed: int = 0) -> dict:
    streams_of = jax.random.split(jax.random.key(seed), 8)
    return {
        "stored_layer_input": noise(streams_of[0], (TOKENS, MODEL_WIDTH), 1.0, 6.0, ((0, 16), (1, 16))),
        "saved_up_output": noise(streams_of[1], (TOKENS, HIDDEN_UNITS), 1.0, 6.0, ((0, 16), (1, 16))),
        "hidden_gradient": noise(streams_of[2], (TOKENS, HIDDEN_UNITS), 1.0, 6.0, ((0, 16), (1, 16))),
        "frozen_gate_weight": draw_frozen_gate_weight(jax.random.fold_in(streams_of[7], 71), 0),
        "lowrank_down": noise(streams_of[4], (MODEL_WIDTH, ADAPTER_RANK), MODEL_WIDTH ** -0.5, 0.09375),
        "lowrank_up": noise(streams_of[5], (ADAPTER_RANK, HIDDEN_UNITS), ADAPTER_RANK ** -0.5, 0.75, ((1, 16),)),
        "magnitude": jnp.clip(jnp.exp(math.log(4.0) - 2.0794415 * jax.random.uniform(streams_of[6], (HIDDEN_UNITS,), jnp.float32) ** steps_of(streams_of[6], (HIDDEN_UNITS,), ((0, 16),), -0.2, 0.2)), 0.5, 4.0),
    }


epsilon = 1e-06

def contract(left, right, left_dim, right_dim, precision=None):
    return lax.dot_general(left, right, (((left_dim,), (right_dim,)), ((), ())), precision=precision, preferred_element_type=jnp.float32)

def reference(stored_layer_input, saved_up_output, hidden_gradient, frozen_gate_weight, lowrank_down, lowrank_up, magnitude):
    combined_weight_matrix = frozen_gate_weight.astype(jnp.float32) + contract(lowrank_down, lowrank_up, 1, 0)
    col_norms = jnp.sqrt(lax.optimization_barrier(jnp.sum(combined_weight_matrix * combined_weight_matrix, axis=0)) + epsilon)
    scales = magnitude / col_norms
    merged = combined_weight_matrix.astype(jnp.bfloat16)
    gate_pre = contract(stored_layer_input, merged, 1, 0)
    gate_out = gate_pre * scales
    gate_sig = jax.nn.sigmoid(gate_out)
    cotangent = hidden_gradient.astype(jnp.float32)
    up_output_gradient = (cotangent * gate_out * gate_sig).astype(jnp.bfloat16)
    gate_grad = cotangent * saved_up_output.astype(jnp.float32) * gate_sig * (1.0 + gate_out * (1.0 - gate_sig))
    scaling_factor = 1.0 / math.sqrt(TOKENS)
    magnitude_gradient = lax.optimization_barrier(jnp.sum(gate_grad * gate_pre, axis=0)) / col_norms * scaling_factor
    scaled_gradient = (gate_grad * scales).astype(jnp.bfloat16)
    layer_input_gradient = contract(scaled_gradient, merged, 1, 1).astype(jnp.bfloat16)
    lowrank_query = contract(scaled_gradient, lowrank_up, 1, 1)
    lowrank_latent = contract(stored_layer_input, lowrank_down, 1, 0)
    lowrank_down_gradient = contract(stored_layer_input.astype(jnp.float32), lowrank_query, 0, 0, lax.Precision.HIGHEST) * scaling_factor
    lowrank_up_gradient = contract(lowrank_latent, scaled_gradient.astype(jnp.float32), 0, 0, lax.Precision.HIGHEST) * scaling_factor
    return (layer_input_gradient, up_output_gradient, lowrank_down_gradient, lowrank_up_gradient, magnitude_gradient)
```

```python
import functools
import math

import jax
import jax.numpy as jnp
from jax import lax
from jax.experimental import pallas as pl
from jax.experimental.pallas import tpu as pltpu
from jax.sharding import PartitionSpec as P

EPSILON = 1e-06
RING = 8
PAIR = 2

EARLY = (
    (0, 0),
    (0, -1), (0, 1), (1, 0),
    (0, -2), (0, 2), (1, -1),
    (0, -3), (0, 3), (1, 1),
    (0, 4), (1, 2), (1, -2),
)
LATE = ((1, -3), (1, 3), (1, 4))
FIRST_OUT = ((1, 4), (1, -3), (1, 3))
REST_OUT = (
    (0, 4), (1, 2), (1, -2), (0, -3), (0, 3), (1, 1), (0, -2), (0, 2), (1, -1),
    (0, -1), (0, 1), (1, 0), (0, 0),
)

ANY = pl.BlockSpec(memory_space=pl.ANY)
VMEM = pl.BlockSpec(memory_space=pltpu.VMEM)
SMEM = pl.BlockSpec(memory_space=pltpu.SMEM)


def ring_perm(step):
    return [
        (pair * RING + at, pair * RING + (at + step) % RING)
        for pair in range(PAIR)
        for at in range(RING)
    ]


def ring_xor(bit):
    return [
        (pair * RING + at, pair * RING + (at ^ bit)) for pair in range(PAIR) for at in range(RING)
    ]


def flip_perm(bit):
    return [(at, at ^ bit) for at in range(16)]


def up_ring(array):
    return lax.ppermute(array, "tensor", ring_perm(1))


def down_ring(array):
    return lax.ppermute(array, "tensor", ring_perm(-1))


def across(array):
    return lax.ppermute(array, "tensor", flip_perm(RING))


def dot(left, right, left_dim, right_dim):
    return lax.dot_general(
        left, right, (((left_dim,), (right_dim,)), ((), ())), preferred_element_type=jnp.float32
    )


def row_of(rank, offset, height):
    pair, ring = offset
    own_pair, own_ring = rank // RING, rank % RING
    other = own_pair if pair == 0 else 1 - own_pair
    block = other * RING + (own_ring + ring + RING) % RING
    return pl.multiple_of(block * height, height)


def merge_kernel(weight_ref, down_ref, up_ref, merged_ref, square_ref):
    wide = weight_ref[...].astype(jnp.float32) + dot(down_ref[...], up_ref[...], 1, 0)
    width = wide.shape[1]
    merged_ref[:, :width] = wide.astype(jnp.bfloat16)
    merged_ref[:, width:] = jnp.concatenate(
        [down_ref[...], jnp.zeros_like(down_ref)], axis=1
    )
    part = jnp.sum(wide * wide, axis=0, keepdims=True)

    @pl.when(pl.program_id(0) == 0)
    def _():
        square_ref[...] = part

    @pl.when(pl.program_id(0) != 0)
    def _():
        square_ref[...] += part


def merge(weight, lowrank_down, lowrank_up):
    depth, width = weight.shape
    rank = lowrank_down.shape[1]
    rows = 512
    return pl.pallas_call(
        merge_kernel,
        grid=(depth // rows,),
        in_specs=[
            pl.BlockSpec((rows, width), lambda i: (i, 0)),
            pl.BlockSpec((rows, rank), lambda i: (i, 0)),
            pl.BlockSpec((rank, width), lambda i: (0, 0)),
        ],
        out_specs=[
            pl.BlockSpec((rows, width + 2 * rank), lambda i: (i, 0)),
            pl.BlockSpec((1, width), lambda i: (0, 0)),
        ],
        out_shape=[
            jax.ShapeDtypeStruct((depth, width + 2 * rank), jnp.bfloat16),
            jax.ShapeDtypeStruct((1, width), jnp.float32),
        ],
        compiler_params=pltpu.CompilerParams(vmem_limit_bytes=32 * 2**20),
        cost_estimate=pl.CostEstimate(
            flops=2 * depth * width * rank, bytes_accessed=4 * depth * width, transcendentals=0
        ),
        name="merge",
    )(weight, lowrank_down, lowrank_up)


def gate_early_kernel(count, rank_ref, *refs):
    blocks, merged_ref, total_ref, held, rows, sems = (
        refs[:count], refs[count], refs[count + 1], refs[count + 2], refs[count + 3], refs[count + 4]
    )
    rank = rank_ref[0]
    height = held.shape[2]
    copies = []
    for at, offset in enumerate(EARLY):
        pair = (
            pltpu.make_async_copy(blocks[at], held.at[at], sems.at[at, 0]),
            pltpu.make_async_copy(
                merged_ref.at[pl.ds(row_of(rank, offset, height), height)],
                rows.at[at],
                sems.at[at, 1],
            ),
        )
        for copy in pair:
            copy.start()
        copies.append(pair)
    for at in range(count):
        for copy in copies[at]:
            copy.wait()
        part = dot(held[at], rows[at], 1, 0)
        if at == 0:
            total_ref[...] = part
        else:
            total_ref[...] += part


def gate_early(rank, blocks, merged):
    tokens, height = blocks[0].shape
    wide = merged.shape[1]
    count = len(blocks)
    return pl.pallas_call(
        functools.partial(gate_early_kernel, count),
        in_specs=[SMEM] + [ANY] * (count + 1),
        out_specs=VMEM,
        out_shape=jax.ShapeDtypeStruct((tokens, wide), jnp.float32),
        scratch_shapes=[
            pltpu.VMEM((count, tokens, height), jnp.bfloat16),
            pltpu.VMEM((count, height, wide), jnp.bfloat16),
            pltpu.SemaphoreType.DMA((count, 2)),
        ],
        compiler_params=pltpu.CompilerParams(vmem_limit_bytes=40 * 2**20),
        cost_estimate=pl.CostEstimate(
            flops=2 * tokens * height * wide * count,
            bytes_accessed=count * height * (wide + tokens) * 2 + tokens * wide * 4,
            transcendentals=0,
        ),
        name="gate_early",
    )(rank, *blocks, merged)


def gate_late_kernel(
    factor,
    rank_ref,
    late_a,
    late_b,
    late_c,
    merged_ref,
    total_ref,
    square_ref,
    magnitude_ref,
    hidden_ref,
    saved_ref,
    lowrank_up_ref,
    up_out_ref,
    scaled_ref,
    query_ref,
    up_piece_ref,
    magnitude_piece_ref,
    first_a,
    first_b,
    first_c,
    held,
    rows,
    out_rows,
    sems,
):
    rank = rank_ref[0]
    height = held.shape[2]
    width = hidden_ref.shape[1]
    low = lowrank_up_ref.shape[0]
    copies = []
    for at, (block, offset) in enumerate(zip((late_a, late_b, late_c), LATE)):
        pair = (
            pltpu.make_async_copy(block, held.at[at], sems.at[at, 0]),
            pltpu.make_async_copy(
                merged_ref.at[pl.ds(row_of(rank, offset, height), height)],
                rows.at[at],
                sems.at[at, 1],
            ),
        )
        for copy in pair:
            copy.start()
        copies.append(pair)
    out_copies = []
    for at, offset in enumerate(FIRST_OUT):
        copy = pltpu.make_async_copy(
            merged_ref.at[pl.ds(row_of(rank, offset, height), height)],
            out_rows.at[at],
            sems.at[at, 2],
        )
        copy.start()
        out_copies.append(copy)
    for at in range(len(LATE)):
        for copy in copies[at]:
            copy.wait()
    norms = jnp.sqrt(square_ref[...] + EPSILON)
    scales = magnitude_ref[...] / norms
    tokens = hidden_ref.shape[0]
    tile = 128

    magnitude_piece_ref[...] = jnp.zeros_like(magnitude_piece_ref)
    up_piece_ref[...] = jnp.zeros_like(up_piece_ref)

    @pl.loop(0, tokens // tile)
    def _(step):
        here = pl.ds(pl.multiple_of(step * tile, tile), tile)
        total = total_ref[here, :]
        for at in range(len(LATE)):
            total += dot(held[at, here, :], rows[at], 1, 0)
        gate_pre = total[:, :width]
        latent = total[:, width : width + low]
        gate_out = gate_pre * scales
        gate_sig = 1.0 / (1.0 + jnp.exp(-gate_out))
        cotangent = hidden_ref[here, :].astype(jnp.float32)
        up_out_ref[here, :] = (cotangent * gate_out * gate_sig).astype(jnp.bfloat16)
        gate_grad = (
            cotangent
            * saved_ref[here, :].astype(jnp.float32)
            * gate_sig
            * (1.0 + gate_out * (1.0 - gate_sig))
        )
        magnitude_piece_ref[...] += jnp.sum(gate_grad * gate_pre, axis=0, keepdims=True)
        scaled = (gate_grad * scales).astype(jnp.bfloat16)
        scaled_ref[here, :] = scaled
        latent_high = latent.astype(jnp.bfloat16)
        latent_rest = (latent - latent_high.astype(jnp.float32)).astype(jnp.bfloat16)
        up_piece_ref[...] += dot(latent_high, scaled, 0, 0) + dot(latent_rest, scaled, 0, 0)

    magnitude_piece_ref[...] = magnitude_piece_ref[...] / norms * factor
    up_piece_ref[...] = up_piece_ref[...] * factor
    for at, out in enumerate((first_a, first_b, first_c)):
        out_copies[at].wait()
        out[...] = dot(scaled_ref[...], out_rows[at][:, :width], 1, 1).astype(jnp.bfloat16)
    query_ref[...] = dot(lowrank_up_ref[...], scaled_ref[...], 1, 1).astype(jnp.bfloat16)


def gate_late(factor, rank, late, merged, total, square, magnitude, hidden, saved, lowrank_up):
    tokens, height = late[0].shape
    wide = merged.shape[1]
    width = hidden.shape[1]
    low = lowrank_up.shape[0]
    block = jax.ShapeDtypeStruct((tokens, height), jnp.bfloat16)
    return pl.pallas_call(
        functools.partial(gate_late_kernel, factor),
        in_specs=[SMEM] + [ANY] * 4 + [VMEM] * 6,
        out_specs=[VMEM] * 8,
        out_shape=[
            jax.ShapeDtypeStruct((tokens, width), jnp.bfloat16),
            jax.ShapeDtypeStruct((tokens, width), jnp.bfloat16),
            jax.ShapeDtypeStruct((low, tokens), jnp.bfloat16),
            jax.ShapeDtypeStruct((low, width), jnp.float32),
            jax.ShapeDtypeStruct((1, width), jnp.float32),
            block,
            block,
            block,
        ],
        scratch_shapes=[
            pltpu.VMEM((len(LATE), tokens, height), jnp.bfloat16),
            pltpu.VMEM((len(LATE), height, wide), jnp.bfloat16),
            pltpu.VMEM((len(LATE), height, wide), jnp.bfloat16),
            pltpu.SemaphoreType.DMA((len(LATE), 3)),
        ],
        compiler_params=pltpu.CompilerParams(vmem_limit_bytes=40 * 2**20),
        cost_estimate=pl.CostEstimate(
            flops=2 * tokens * height * wide * 7,
            bytes_accessed=16 * 2**20,
            transcendentals=2 * tokens * width,
        ),
        name="gate_late",
    )(rank, *late, merged, total, square, magnitude, hidden, saved, lowrank_up)


def rest_kernel(count, rank_ref, merged_ref, scaled_ref, *refs):
    outs, rows, sems = refs[:count], refs[count], refs[count + 1]
    rank = rank_ref[0]
    height = rows.shape[1]
    width = scaled_ref.shape[1]
    copies = []
    for at, offset in enumerate(REST_OUT):
        copy = pltpu.make_async_copy(
            merged_ref.at[pl.ds(row_of(rank, offset, height), height)], rows.at[at], sems.at[at]
        )
        copy.start()
        copies.append(copy)
    for at in range(count):
        copies[at].wait()
        outs[at][...] = dot(scaled_ref[...], rows[at][:, :width], 1, 1).astype(jnp.bfloat16)


def rest(rank, merged, scaled, height):
    tokens, width = scaled.shape
    wide = merged.shape[1]
    count = len(REST_OUT)
    return pl.pallas_call(
        functools.partial(rest_kernel, count),
        in_specs=[SMEM, ANY, VMEM],
        out_specs=[VMEM] * count,
        out_shape=[jax.ShapeDtypeStruct((tokens, height), jnp.bfloat16)] * count,
        scratch_shapes=[
            pltpu.VMEM((count, height, wide), jnp.bfloat16),
            pltpu.SemaphoreType.DMA((count,)),
        ],
        compiler_params=pltpu.CompilerParams(vmem_limit_bytes=40 * 2**20),
        cost_estimate=pl.CostEstimate(
            flops=2 * tokens * height * width * count,
            bytes_accessed=count * height * (wide + tokens) * 2,
            transcendentals=0,
        ),
        name="rest",
    )(rank, merged, scaled)


def payload_kernel(factor, query_ref, input_ref, up_ref, magnitude_ref, out_ref):
    query = query_ref[...]
    high = query.astype(jnp.bfloat16)
    rest_part = (query - high.astype(jnp.float32)).astype(jnp.bfloat16)
    low, width = up_ref.shape
    down = (dot(high, input_ref[...], 1, 0) + dot(rest_part, input_ref[...], 1, 0)) * factor
    out_ref[...] = jnp.zeros_like(out_ref)
    out_ref[:low, :width] = up_ref[...]
    out_ref[:low, width:] = down
    out_ref[low : low + 1, :width] = magnitude_ref[...]


def payload(factor, query, own, up_piece, magnitude_piece):
    low, width = up_piece.shape
    return pl.pallas_call(
        functools.partial(payload_kernel, factor),
        in_specs=[VMEM] * 4,
        out_specs=VMEM,
        out_shape=jax.ShapeDtypeStruct((low + 8, width + own.shape[1]), jnp.float32),
        cost_estimate=pl.CostEstimate(
            flops=4 * low * own.shape[0] * own.shape[1], bytes_accessed=2**20, transcendentals=0
        ),
        name="payload",
    )(query, own, up_piece, magnitude_piece)


def f32(array):
    return array.astype(jnp.float32)


def narrow(*arrays):
    total = f32(arrays[0])
    for array in arrays[1:]:
        total = total + f32(array)
    return total.astype(jnp.bfloat16)


def sum_small(array, perms, axis):
    for perm in perms:
        sent = lax.optimization_barrier(array.astype(jnp.bfloat16))
        array = f32(sent) + f32(lax.ppermute(sent, axis, perm))
    return array


def sum_payload(array, perms, low):
    array = array + lax.ppermute(array, "dp", flip_perm(1))
    for perm in perms:
        row = array[low : low + 1]
        high = lax.reduce_precision(row, 8, 7)
        pad = jnp.zeros((14, array.shape[1]), jnp.float32)
        sent = jnp.concatenate([array[:low], high, row - high, pad], axis=0).astype(jnp.bfloat16)
        sent = lax.optimization_barrier(sent)
        both = f32(sent) + f32(lax.ppermute(sent, "dp", perm))
        array = jnp.concatenate([both[:low], both[low : low + 1] + both[low + 1 : low + 2]], axis=0)
    return array


def per_device(
    stored_layer_input,
    saved_up_output,
    hidden_gradient,
    frozen_gate_weight,
    lowrank_down,
    lowrank_up,
    magnitude,
):
    own = stored_layer_input
    tokens, height = own.shape
    width = frozen_gate_weight.shape[1]
    low = lowrank_up.shape[0]
    factor = 1.0 / math.sqrt(tokens * lax.axis_size("dp"))
    rank = lax.axis_index("tensor").astype(jnp.int32).reshape(1)

    merged, square = merge(frozen_gate_weight, lowrank_down, lowrank_up)

    got = {(0, 0): own}
    got[0, -1], got[0, 1], got[1, 0] = up_ring(own), down_ring(own), across(own)
    got[0, -2], got[0, 2], got[1, -1] = (
        up_ring(got[0, -1]), down_ring(got[0, 1]), across(got[0, -1])
    )
    got[0, -3], got[0, 3], got[1, 1] = (
        up_ring(got[0, -2]), down_ring(got[0, 2]), across(got[0, 1])
    )
    got[0, 4], got[1, 2], got[1, -2] = (
        up_ring(got[0, -3]), down_ring(got[1, 1]), across(got[0, -2])
    )
    got[1, -3], got[1, 3], got[1, 4] = (
        up_ring(got[1, -2]), down_ring(got[1, 2]), across(got[0, 4])
    )

    total = gate_early(rank, [got[offset] for offset in EARLY], merged)
    up_output_gradient, scaled, query, up_piece, magnitude_piece, *first = gate_late(
        factor,
        rank,
        [got[offset] for offset in LATE],
        merged,
        total,
        square,
        magnitude.reshape(1, width),
        hidden_gradient,
        saved_up_output,
        lowrank_up,
    )
    part = dict(zip(FIRST_OUT, first))
    into_far, into_down, into_up = (
        across(part[1, 4]), down_ring(part[1, -3]), up_ring(part[1, 3])
    )
    part.update(zip(REST_OUT, rest(rank, merged, scaled, height)))
    in_a = down_ring(narrow(part[0, 4], into_far))
    in_b = up_ring(narrow(part[1, 2], into_up))
    in_c = across(narrow(part[1, -2], into_down))
    in_d = down_ring(narrow(part[0, -3], in_a))
    in_e = up_ring(part[0, 3])
    in_f = across(narrow(part[1, 1], in_b))
    in_g = down_ring(narrow(part[0, -2], in_c, in_d))
    in_h = up_ring(narrow(part[0, 2], in_e))
    in_i = across(part[1, -1])
    in_j = down_ring(narrow(part[0, -1], in_g, in_i))
    in_k = up_ring(narrow(part[0, 1], in_f, in_h))
    in_l = across(part[1, 0])
    layer_input_gradient = narrow(part[0, 0], in_j, in_k, in_l)

    query = sum_small(query, (flip_perm(RING), ring_xor(1), ring_xor(2), ring_xor(4)), "tensor")
    pieces = payload(factor, query, own, up_piece, magnitude_piece)
    summed = sum_payload(pieces, (flip_perm(2), flip_perm(4), flip_perm(8)), low)
    return (
        layer_input_gradient,
        up_output_gradient,
        jnp.transpose(summed[:low, width:]),
        summed[:low, :width],
        summed[low, :width],
    )


def solution(mesh):
    return jax.shard_map(
        per_device,
        mesh=mesh,
        in_specs=(
            P("dp", "tensor"),
            P("dp", "tensor"),
            P("dp", "tensor"),
            P(None, "tensor"),
            P(),
            P(None, "tensor"),
            P("tensor"),
        ),
        out_specs=(
            P("dp", "tensor"),
            P("dp", "tensor"),
            P("tensor", None),
            P(None, "tensor"),
            P("tensor"),
        ),
        check_vma=False,
    )
```

```python
import functools
import math

import jax
import jax.numpy as jnp
from jax import lax
from jax.experimental import pallas as pl
from jax.experimental.pallas import tpu as pltpu
from jax.sharding import PartitionSpec as P

EPSILON = 1e-06
RING = 8
PAIR = 2
MERGE_ROWS = 512

EARLY = (
    (0, 0),
    (0, -1), (0, 1), (1, 0),
    (0, -2), (0, 2), (1, -1),
    (0, -3), (0, 3), (1, 1),
    (0, 4), (1, 2), (1, -2),
)
LATE = ((1, -3), (1, 3), (1, 4))
REST_OUT = (
    (0, 4), (1, 2), (1, -2), (0, -3), (0, 3), (1, 1), (0, -2), (0, 2), (1, -1),
    (0, -1), (0, 1), (1, 0), (0, 0),
)

VMEM = pl.BlockSpec(memory_space=pltpu.VMEM)
SMEM = pl.BlockSpec(memory_space=pltpu.SMEM)


def ring_perm(step):
    pairs = []
    for group in range(16):
        move = -step if group % 2 else step
        for pair in range(PAIR):
            for at in range(RING):
                source = (group * PAIR + pair) * RING + at
                pairs.append((source, source - at + (at + move) % RING))
    return pairs


def xor_perm(bits):
    return [(at, at ^ bits) for at in range(16)]


def up_ring(array):
    return lax.ppermute(array, ("dp", "tensor"), ring_perm(1))


def down_ring(array):
    return lax.ppermute(array, ("dp", "tensor"), ring_perm(-1))


def across(array):
    return lax.ppermute(array, "tensor", xor_perm(RING))


def dot(left, right, left_dim, right_dim):
    return lax.dot_general(
        left, right, (((left_dim,), (right_dim,)), ((), ())), preferred_element_type=jnp.float32
    )


def row_of(rank, offset, height, sign):
    pair, ring = offset
    ring = ring * sign
    own_pair, own_ring = rank // RING, rank % RING
    other = own_pair if pair == 0 else 1 - own_pair
    block = other * RING + (own_ring + ring + RING) % RING
    return pl.multiple_of(block * height, height)


def merge_rows(first, parts, weight_ref, down_ref, up_ref, merged_ref, square_ref):
    width = weight_ref.shape[1]

    @pl.loop(first, first + parts)
    def _(part):
        here = pl.ds(pl.multiple_of(part * MERGE_ROWS, MERGE_ROWS), MERGE_ROWS)
        down = down_ref[:, here]
        wide = weight_ref[here, :].astype(jnp.float32) + dot(down, up_ref[...], 0, 0)
        merged_ref[here, :width] = wide.astype(jnp.bfloat16)
        merged_ref[here, width:] = jnp.concatenate([down, jnp.zeros_like(down)], axis=0).T
        square_ref[...] += jnp.sum(wide * wide, axis=0, keepdims=True)


def merge_head_kernel(parts, weight_ref, down_ref, up_ref, merged_ref, square_ref):
    square_ref[...] = jnp.zeros_like(square_ref)
    merge_rows(0, parts, weight_ref, down_ref, up_ref, merged_ref, square_ref)


def merge_tail_kernel(
    first, parts, weight_ref, down_ref, up_ref, head_ref, head_square_ref, merged_ref, square_ref
):
    square_ref[...] = head_square_ref[...]
    merge_rows(first, parts, weight_ref, down_ref, up_ref, merged_ref, square_ref)


def merge(first, parts, operands, head):
    weight, down_t, _ = operands
    depth, width = weight.shape
    rank = down_t.shape[0]
    rows = parts * MERGE_ROWS
    if head:
        kernel, aliases = functools.partial(merge_tail_kernel, first, parts), {3: 0}
    else:
        kernel, aliases = functools.partial(merge_head_kernel, parts), {}
    return pl.pallas_call(
        kernel,
        in_specs=[VMEM] * (3 + len(head)),
        out_specs=[VMEM] * 2,
        out_shape=[
            jax.ShapeDtypeStruct((depth, width + 2 * rank), jnp.bfloat16),
            jax.ShapeDtypeStruct((1, width), jnp.float32),
        ],
        input_output_aliases=aliases,
        compiler_params=pltpu.CompilerParams(vmem_limit_bytes=6 * 2**20),
        cost_estimate=pl.CostEstimate(
            flops=2 * rows * width * rank, bytes_accessed=4 * rows * width, transcendentals=0
        ),
        name="merge_tail" if head else "merge_head",
    )(*operands, *head)


def split(array):
    high = array.astype(jnp.bfloat16)
    low = (array - high.astype(jnp.float32)).astype(jnp.bfloat16)
    return jnp.concatenate([high, low], axis=0)


def gradient_block(scaled_ref, rows, both_ref, block_ref, out_ref):
    tokens = scaled_ref.shape[0]
    low = both_ref.shape[0] // 2
    out_ref[:tokens, :] = dot(scaled_ref[...], rows, 1, 1).astype(jnp.bfloat16)
    down = dot(both_ref[...], block_ref[...], 1, 0)
    out_ref[tokens:, :] = (down[:low] + down[low:]).astype(jnp.bfloat16)


def gate_early_kernel(count, rank_ref, *refs):
    blocks, merged_ref, total_ref = refs[:count], refs[count], refs[count + 1]
    rank, sign = rank_ref[0], rank_ref[1]
    height = blocks[0].shape[1]
    for at, offset in enumerate(EARLY):
        rows = merged_ref[pl.ds(row_of(rank, offset, height, sign), height), :]
        part = dot(blocks[at][...], rows, 1, 0)
        if at == 0:
            total_ref[...] = part
        else:
            total_ref[...] += part


def gate_early(rank, blocks, merged):
    tokens, height = blocks[0].shape
    wide = merged.shape[1]
    count = len(blocks)
    return pl.pallas_call(
        functools.partial(gate_early_kernel, count),
        in_specs=[SMEM] + [VMEM] * (count + 1),
        out_specs=VMEM,
        out_shape=jax.ShapeDtypeStruct((tokens, wide), jnp.float32),
        compiler_params=pltpu.CompilerParams(vmem_limit_bytes=6 * 2**20),
        cost_estimate=pl.CostEstimate(
            flops=2 * tokens * height * wide * count,
            bytes_accessed=count * height * (wide + tokens) * 2 + tokens * wide * 4,
            transcendentals=0,
        ),
        name="gate_early",
    )(rank, *blocks, merged)


def gate_late_kernel(
    factor,
    rank_ref,
    late_a,
    late_b,
    late_c,
    merged_ref,
    total_ref,
    square_ref,
    magnitude_ref,
    hidden_ref,
    saved_ref,
    lowrank_up_ref,
    up_out_ref,
    scaled_ref,
    both_ref,
    latent_ref,
    magnitude_piece_ref,
    first_a,
    first_b,
    first_c,
):
    rank, sign = rank_ref[0], rank_ref[1]
    tokens, height = late_a.shape
    width = hidden_ref.shape[1]
    low = lowrank_up_ref.shape[0]
    norms = jnp.sqrt(square_ref[...] + EPSILON)
    scales = magnitude_ref[...] / norms
    tile = 128
    starts = [row_of(rank, offset, height, sign) for offset in LATE]
    magnitude_piece_ref[...] = jnp.zeros_like(magnitude_piece_ref)

    @pl.loop(0, tokens // tile)
    def _(step):
        here = pl.ds(pl.multiple_of(step * tile, tile), tile)
        total = total_ref[here, :]
        for block, start in zip((late_a, late_b, late_c), starts):
            total += dot(block[here, :], merged_ref[pl.ds(start, height), :], 1, 0)
        gate_pre = total[:, :width]
        latent = total[:, width : width + low]
        gate_out = gate_pre * scales
        gate_sig = 1.0 / (1.0 + jnp.exp(-gate_out))
        cotangent = hidden_ref[here, :].astype(jnp.float32)
        up_out_ref[here, :] = (cotangent * gate_out * gate_sig).astype(jnp.bfloat16)
        gate_grad = (
            cotangent
            * saved_ref[here, :].astype(jnp.float32)
            * gate_sig
            * (1.0 + gate_out * (1.0 - gate_sig))
        )
        magnitude_piece_ref[...] += jnp.sum(gate_grad * gate_pre, axis=0, keepdims=True)
        scaled_ref[here, :] = (gate_grad * scales).astype(jnp.bfloat16)
        latent_high = latent.astype(jnp.bfloat16)
        latent_rest = (latent - latent_high.astype(jnp.float32)).astype(jnp.bfloat16)
        latent_ref[here, :] = jnp.concatenate([latent_high, latent_rest], axis=1)

    magnitude_piece_ref[...] = magnitude_piece_ref[...] / norms * factor
    both_ref[...] = split(dot(lowrank_up_ref[...], scaled_ref[...], 1, 1))
    for offset, block, out in zip(LATE, (late_a, late_b, late_c), (first_a, first_b, first_c)):
        rows = merged_ref[pl.ds(row_of(rank, offset, height, sign), height), :width]
        gradient_block(scaled_ref, rows, both_ref, block, out)


def gate_late(factor, rank, late, merged, total, square, magnitude, hidden, saved, lowrank_up):
    tokens, height = late[0].shape
    wide = merged.shape[1]
    width = hidden.shape[1]
    low = lowrank_up.shape[0]
    block = jax.ShapeDtypeStruct((tokens + low, height), jnp.bfloat16)
    return pl.pallas_call(
        functools.partial(gate_late_kernel, factor),
        in_specs=[SMEM] + [VMEM] * 10,
        out_specs=[VMEM] * 8,
        out_shape=[
            jax.ShapeDtypeStruct((tokens, width), jnp.bfloat16),
            jax.ShapeDtypeStruct((tokens, width), jnp.bfloat16),
            jax.ShapeDtypeStruct((2 * low, tokens), jnp.bfloat16),
            jax.ShapeDtypeStruct((tokens, 2 * low), jnp.bfloat16),
            jax.ShapeDtypeStruct((1, width), jnp.float32),
            block,
            block,
            block,
        ],
        compiler_params=pltpu.CompilerParams(vmem_limit_bytes=6 * 2**20),
        cost_estimate=pl.CostEstimate(
            flops=2 * tokens * height * wide * 7,
            bytes_accessed=8 * 2**20,
            transcendentals=2 * tokens * width,
        ),
        name="gate_late",
    )(rank, *late, merged, total, square, magnitude, hidden, saved, lowrank_up)


def rest_kernel(factor, count, rank_ref, merged_ref, scaled_ref, latent_ref, both_ref, *refs):
    blocks, up_piece_ref, outs = refs[:count], refs[count], refs[count + 1 :]
    rank, sign = rank_ref[0], rank_ref[1]
    height = outs[0].shape[1]
    low, width = up_piece_ref.shape
    for offset, block, out in zip(REST_OUT, blocks, outs):
        rows = merged_ref[pl.ds(row_of(rank, offset, height, sign), height), :width]
        gradient_block(scaled_ref, rows, both_ref, block, out)
    both = dot(latent_ref[...], scaled_ref[...], 0, 0)
    up_piece_ref[...] = (both[:low] + both[low:]) * factor


def rest(factor, rank, merged, scaled, latent, both, blocks):
    tokens, width = scaled.shape
    height = blocks[0].shape[1]
    wide = merged.shape[1]
    count = len(REST_OUT)
    low = latent.shape[1] // 2
    return pl.pallas_call(
        functools.partial(rest_kernel, factor, count),
        in_specs=[SMEM] + [VMEM] * (4 + count),
        out_specs=[VMEM] * (count + 1),
        out_shape=[jax.ShapeDtypeStruct((low, width), jnp.float32)]
        + [jax.ShapeDtypeStruct((tokens + low, height), jnp.bfloat16)] * count,
        compiler_params=pltpu.CompilerParams(vmem_limit_bytes=6 * 2**20),
        cost_estimate=pl.CostEstimate(
            flops=2 * tokens * height * width * count,
            bytes_accessed=count * height * (wide + tokens) * 2,
            transcendentals=0,
        ),
        name="rest",
    )(rank, merged, scaled, latent, both, *blocks)


def payload_kernel(factor, tokens, rank_ref, up_ref, magnitude_ref, *refs):
    parts, (kept_ref, sent_ref) = refs[:4], refs[4:]
    low, width = up_ref.shape
    half = low // 2
    core = rank_ref[2]
    for out, upper in ((kept_ref, core), (sent_ref, 1 - core)):
        first = upper == 0
        here = pl.ds(pl.multiple_of(tokens + upper * half, half), half)
        down = sum(part[here, :].astype(jnp.float32) for part in parts) * factor
        out[...] = jnp.zeros_like(out)
        out[:half, :width] = jnp.where(first, up_ref[:half, :], up_ref[half:, :])
        out[:half, width:] = down
        out[half : half + 1, :width] = magnitude_ref[...]


def payload(factor, tokens, rank, up_piece, magnitude_piece, parts):
    low, width = up_piece.shape
    out = jax.ShapeDtypeStruct((low // 2 + 8, width + parts[0].shape[1]), jnp.float32)
    return pl.pallas_call(
        functools.partial(payload_kernel, factor, tokens),
        in_specs=[SMEM] + [VMEM] * 6,
        out_specs=[VMEM] * 2,
        out_shape=[out] * 2,
        compiler_params=pltpu.CompilerParams(vmem_limit_bytes=6 * 2**20),
        cost_estimate=pl.CostEstimate(flops=2**20, bytes_accessed=2**20, transcendentals=0),
        name="payload",
    )(rank, up_piece, magnitude_piece, *parts)


def f32(array):
    return array.astype(jnp.float32)


def narrow(*arrays):
    total = f32(arrays[0])
    for array in arrays[1:]:
        total = total + f32(array)
    return total.astype(jnp.bfloat16)


def sum_four(array, axis, bits):
    sent = lax.optimization_barrier(array.astype(jnp.bfloat16))
    one, two = bits
    near, far, both = (lax.ppermute(sent, axis, xor_perm(at)) for at in (one, two, one ^ two))
    return (f32(sent) + f32(near)) + (f32(far) + f32(both))


def pack(array, half):
    row = array[half : half + 1]
    high = lax.reduce_precision(row, 8, 7)
    pad = jnp.zeros((14, array.shape[1]), jnp.float32)
    return jnp.concatenate([array[:half], high, row - high, pad], axis=0)


def unpack(array, half):
    return jnp.concatenate(
        [array[:half], array[half : half + 1] + array[half + 1 : half + 2]], axis=0
    )


def together(*arrays):
    return lax.optimization_barrier(arrays)


def per_device(
    stored_layer_input,
    saved_up_output,
    hidden_gradient,
    frozen_gate_weight,
    lowrank_down,
    lowrank_up,
    magnitude,
):
    own = stored_layer_input
    tokens, height = own.shape
    width = frozen_gate_weight.shape[1]
    low = lowrank_up.shape[0]
    factor = 1.0 / math.sqrt(tokens * lax.axis_size("dp"))
    core = lax.axis_index("dp") % 2
    rank = jnp.stack([lax.axis_index("tensor"), 1 - 2 * core, core]).astype(jnp.int32)
    rank, magnitude_row, own = together(rank, magnitude.reshape(1, width), own)

    operands = (frozen_gate_weight, jnp.transpose(lowrank_down), lowrank_up)
    head = merge(0, 2, operands, ())

    got = {(0, 0): own}
    token = own[:16, :128]

    def arrive(move, source, target, *more):
        nonlocal token
        block = move(got[source])
        token, got[target], *more = together(token, block, *more)
        return more

    head = arrive(up_ring, (0, 0), (0, -1), *head)
    arrive(down_ring, (0, 0), (0, 1))
    arrive(across, (0, 0), (1, 0))
    merged, square = merge(2, 6, operands, head)
    merged, square = arrive(up_ring, (0, -1), (0, -2), merged, square)
    arrive(down_ring, (0, 1), (0, 2))
    arrive(across, (0, -1), (1, -1))
    arrive(up_ring, (0, -2), (0, -3))
    arrive(down_ring, (0, 2), (0, 3))
    arrive(across, (0, 1), (1, 1))
    arrive(up_ring, (0, -3), (0, 4))
    arrive(down_ring, (1, 1), (1, 2))
    arrive(across, (0, -2), (1, -2))
    total = gate_early(rank, [got[offset] for offset in EARLY], merged)
    (total,) = arrive(up_ring, (1, -2), (1, -3), total)
    arrive(down_ring, (1, 2), (1, 3))
    arrive(across, (0, 4), (1, 4))
    *late, total = together(*[got[offset] for offset in LATE], total)

    up_output_gradient, scaled, both, latent, magnitude_piece, *first = gate_late(
        factor,
        rank,
        late,
        merged,
        total,
        square,
        magnitude_row,
        hidden_gradient,
        saved_up_output,
        lowrank_up,
    )
    lower, upper, far = down_ring(first[0]), up_ring(first[1]), across(first[2])
    up_piece, *others = rest(
        factor, rank, merged, scaled, latent, both, [got[offset] for offset in REST_OUT]
    )
    far, lower, upper, up_piece, *others = together(far, lower, upper, up_piece, *others)
    part = dict(zip(REST_OUT, others))

    in_a = down_ring(narrow(part[0, 4], far))
    in_b = up_ring(narrow(part[1, 2], upper))
    in_c = across(narrow(part[1, -2], lower))
    in_a, in_b, in_c = together(in_a, in_b, in_c)

    in_d = down_ring(narrow(part[0, -3], in_a))
    in_e = up_ring(part[0, 3])
    in_f = across(narrow(part[1, 1], in_b))
    in_d, in_e, in_f = together(in_d, in_e, in_f)

    in_g = down_ring(narrow(part[0, -2], in_c, in_d))
    in_h = up_ring(narrow(part[0, 2], in_e))
    in_i = across(part[1, -1])
    in_g, in_h, in_i = together(in_g, in_h, in_i)

    in_j = down_ring(narrow(part[0, -1], in_g, in_i))
    in_k = up_ring(narrow(part[0, 1], in_f, in_h))
    in_l = across(part[1, 0])
    in_j, in_k, in_l = together(in_j, in_k, in_l)
    layer_input_gradient = narrow(*[one[:tokens] for one in (part[0, 0], in_j, in_k, in_l)])

    half = low // 2
    kept, sent = payload(
        factor, tokens, rank, up_piece, magnitude_piece, (part[0, 0], in_j, in_k, in_l)
    )
    pieces = kept + lax.ppermute(sent, "dp", xor_perm(1))
    pieces = unpack(sum_four(pack(pieces, half), "dp", (2, 4)), half)
    sent = lax.optimization_barrier(pack(pieces, half).astype(jnp.bfloat16))
    pieces = unpack(f32(sent) + f32(lax.ppermute(sent, "dp", xor_perm(8))), half)
    mine = pieces[:half]
    other = lax.ppermute(mine, "dp", xor_perm(1))
    summed = jnp.where(
        core == 0,
        jnp.concatenate([mine, other], axis=0),
        jnp.concatenate([other, mine], axis=0),
    )
    return (
        layer_input_gradient,
        up_output_gradient,
        jnp.transpose(summed[:, width:]),
        summed[:, :width],
        pieces[half, :width],
    )


def solution(mesh):
    return jax.shard_map(
        per_device,
        mesh=mesh,
        in_specs=(
            P("dp", "tensor"),
            P("dp", "tensor"),
            P("dp", "tensor"),
            P(None, "tensor"),
            P(),
            P(None, "tensor"),
            P("tensor"),
        ),
        out_specs=(
            P("dp", "tensor"),
            P("dp", "tensor"),
            P("tensor", None),
            P(None, "tensor"),
            P("tensor"),
        ),
        check_vma=False,
    )
```

```python
import functools
import math

import jax
import jax.numpy as jnp
from jax import lax
from jax.experimental import pallas as pl
from jax.experimental.pallas import tpu as pltpu
from jax.sharding import PartitionSpec as P

EPSILON = 1e-06
RING = 8
PAIR = 2
MERGE_ROWS = 512
LANES = 128

EARLY = (
    (0, 0),
    (0, -1), (0, 1), (1, 0),
    (0, -2), (0, 2), (1, -1),
    (0, -3), (0, 3), (1, 1),
    (0, 4), (1, 2), (1, -2),
)
LATE = ((1, -3), (1, 3), (1, 4))
REST_OUT = (
    (0, 4), (1, 2), (1, -2), (0, -3), (0, 3), (1, 1), (0, -2), (0, 2), (1, -1),
    (0, -1), (0, 1), (1, 0), (0, 0),
)

VMEM = pl.BlockSpec(memory_space=pltpu.VMEM)
SMEM = pl.BlockSpec(memory_space=pltpu.SMEM)


def ring_perm(step):
    pairs = []
    for group in range(16):
        move = -step if group % 2 else step
        for pair in range(PAIR):
            for at in range(RING):
                source = (group * PAIR + pair) * RING + at
                pairs.append((source, source - at + (at + move) % RING))
    return pairs


def xor_perm(bits):
    return [(at, at ^ bits) for at in range(16)]


def up_ring(array):
    return lax.ppermute(array, ("dp", "tensor"), ring_perm(1))


def down_ring(array):
    return lax.ppermute(array, ("dp", "tensor"), ring_perm(-1))


def across(array):
    return lax.ppermute(array, "tensor", xor_perm(RING))


def dot(left, right, left_dim, right_dim):
    return lax.dot_general(
        left, right, (((left_dim,), (right_dim,)), ((), ())), preferred_element_type=jnp.float32
    )


def row_of(rank, offset, height, sign):
    pair, ring = offset
    ring = ring * sign
    own_pair, own_ring = rank // RING, rank % RING
    other = own_pair if pair == 0 else 1 - own_pair
    block = other * RING + (own_ring + ring + RING) % RING
    return pl.multiple_of(block * height, height)


def merge_rows(first, parts, weight_ref, down_ref, up_ref, merged_ref, square_ref):
    width = weight_ref.shape[1]

    @pl.loop(first, first + parts)
    def _(part):
        here = pl.ds(pl.multiple_of(part * MERGE_ROWS, MERGE_ROWS), MERGE_ROWS)
        down = down_ref[:, here]
        wide = weight_ref[here, :].astype(jnp.float32) + dot(down, up_ref[...], 0, 0)
        merged_ref[here, :width] = wide.astype(jnp.bfloat16)
        merged_ref[here, width:] = jnp.concatenate([down, jnp.zeros_like(down)], axis=0).T
        square_ref[...] += jnp.sum(wide * wide, axis=0, keepdims=True)


def merge_head_kernel(parts, weight_ref, down_ref, up_ref, merged_ref, square_ref):
    square_ref[...] = jnp.zeros_like(square_ref)
    merge_rows(0, parts, weight_ref, down_ref, up_ref, merged_ref, square_ref)


def merge_tail_kernel(
    first, parts, weight_ref, down_ref, up_ref, head_ref, head_square_ref, merged_ref, square_ref
):
    square_ref[...] = head_square_ref[...]
    merge_rows(first, parts, weight_ref, down_ref, up_ref, merged_ref, square_ref)


def merge(first, parts, operands, head):
    weight, down_t, _ = operands
    depth, width = weight.shape
    rank = down_t.shape[0]
    rows = parts * MERGE_ROWS
    if head:
        kernel, aliases = functools.partial(merge_tail_kernel, first, parts), {3: 0}
    else:
        kernel, aliases = functools.partial(merge_head_kernel, parts), {}
    return pl.pallas_call(
        kernel,
        in_specs=[VMEM] * (3 + len(head)),
        out_specs=[VMEM] * 2,
        out_shape=[
            jax.ShapeDtypeStruct((depth, width + 2 * rank), jnp.bfloat16),
            jax.ShapeDtypeStruct((1, width), jnp.float32),
        ],
        input_output_aliases=aliases,
        compiler_params=pltpu.CompilerParams(vmem_limit_bytes=6 * 2**20),
        cost_estimate=pl.CostEstimate(
            flops=2 * rows * width * rank, bytes_accessed=4 * rows * width, transcendentals=0
        ),
        name="merge_tail" if head else "merge_head",
    )(*operands, *head)


def split(array):
    high = array.astype(jnp.bfloat16)
    low = (array - high.astype(jnp.float32)).astype(jnp.bfloat16)
    return jnp.concatenate([high, low], axis=0)


def gradient_block(scaled_ref, rows, both_ref, block_ref, out_ref):
    tokens = scaled_ref.shape[0]
    low = both_ref.shape[0] // 2
    out_ref[:tokens, :] = dot(scaled_ref[...], rows, 1, 1).astype(jnp.bfloat16)
    down = dot(both_ref[...], block_ref[...], 1, 0)
    out_ref[tokens:, :] = (down[:low] + down[low:]).astype(jnp.bfloat16)


def gate_early_kernel(count, rank_ref, *refs):
    blocks, merged_ref, total_ref = refs[:count], refs[count], refs[count + 1]
    rank, sign = rank_ref[0], rank_ref[1]
    height = blocks[0].shape[1]
    for at, offset in enumerate(EARLY):
        rows = merged_ref[pl.ds(row_of(rank, offset, height, sign), height), :]
        part = dot(blocks[at][...], rows, 1, 0)
        if at == 0:
            total_ref[...] = part
        else:
            total_ref[...] += part


def gate_early(rank, blocks, merged):
    tokens, height = blocks[0].shape
    wide = merged.shape[1]
    count = len(blocks)
    return pl.pallas_call(
        functools.partial(gate_early_kernel, count),
        in_specs=[SMEM] + [VMEM] * (count + 1),
        out_specs=VMEM,
        out_shape=jax.ShapeDtypeStruct((tokens, wide), jnp.float32),
        compiler_params=pltpu.CompilerParams(vmem_limit_bytes=6 * 2**20),
        cost_estimate=pl.CostEstimate(
            flops=2 * tokens * height * wide * count,
            bytes_accessed=count * height * (wide + tokens) * 2 + tokens * wide * 4,
            transcendentals=0,
        ),
        name="gate_early",
    )(rank, *blocks, merged)


def gate_late_kernel(
    factor,
    rank_ref,
    late_a,
    late_b,
    late_c,
    merged_ref,
    total_ref,
    square_ref,
    magnitude_ref,
    hidden_ref,
    saved_ref,
    lowrank_up_ref,
    up_out_ref,
    scaled_ref,
    both_ref,
    latent_ref,
    magnitude_piece_ref,
    first_a,
    first_b,
    first_c,
):
    rank, sign = rank_ref[0], rank_ref[1]
    tokens, height = late_a.shape
    width = hidden_ref.shape[1]
    low = lowrank_up_ref.shape[0]
    norms = jnp.sqrt(square_ref[...] + EPSILON)
    scales = magnitude_ref[...] / norms
    tile = 128
    starts = [row_of(rank, offset, height, sign) for offset in LATE]
    magnitude_piece_ref[...] = jnp.zeros_like(magnitude_piece_ref)

    @pl.loop(0, tokens // tile)
    def _(step):
        here = pl.ds(pl.multiple_of(step * tile, tile), tile)
        total = total_ref[here, :]
        for block, start in zip((late_a, late_b, late_c), starts):
            total += dot(block[here, :], merged_ref[pl.ds(start, height), :], 1, 0)
        gate_pre = total[:, :width]
        latent = total[:, width : width + low]
        gate_out = gate_pre * scales
        gate_sig = 1.0 / (1.0 + jnp.exp(-gate_out))
        cotangent = hidden_ref[here, :].astype(jnp.float32)
        up_out_ref[here, :] = (cotangent * gate_out * gate_sig).astype(jnp.bfloat16)
        gate_grad = (
            cotangent
            * saved_ref[here, :].astype(jnp.float32)
            * gate_sig
            * (1.0 + gate_out * (1.0 - gate_sig))
        )
        magnitude_piece_ref[...] += jnp.sum(gate_grad * gate_pre, axis=0, keepdims=True)
        scaled_ref[here, :] = (gate_grad * scales).astype(jnp.bfloat16)
        latent_high = latent.astype(jnp.bfloat16)
        latent_rest = (latent - latent_high.astype(jnp.float32)).astype(jnp.bfloat16)
        latent_ref[here, :] = jnp.concatenate([latent_high, latent_rest], axis=1)

    magnitude_piece_ref[...] = magnitude_piece_ref[...] / norms * factor
    both_ref[...] = split(dot(lowrank_up_ref[...], scaled_ref[...], 1, 1))
    for offset, block, out in zip(LATE, (late_a, late_b, late_c), (first_a, first_b, first_c)):
        rows = merged_ref[pl.ds(row_of(rank, offset, height, sign), height), :width]
        gradient_block(scaled_ref, rows, both_ref, block, out)


def gate_late(factor, rank, late, merged, total, square, magnitude, hidden, saved, lowrank_up):
    tokens, height = late[0].shape
    wide = merged.shape[1]
    width = hidden.shape[1]
    low = lowrank_up.shape[0]
    block = jax.ShapeDtypeStruct((tokens + low, height), jnp.bfloat16)
    return pl.pallas_call(
        functools.partial(gate_late_kernel, factor),
        in_specs=[SMEM] + [VMEM] * 10,
        out_specs=[VMEM] * 8,
        out_shape=[
            jax.ShapeDtypeStruct((tokens, width), jnp.bfloat16),
            jax.ShapeDtypeStruct((tokens, width), jnp.bfloat16),
            jax.ShapeDtypeStruct((2 * low, tokens), jnp.bfloat16),
            jax.ShapeDtypeStruct((tokens, 2 * low), jnp.bfloat16),
            jax.ShapeDtypeStruct((1, width), jnp.float32),
            block,
            block,
            block,
        ],
        compiler_params=pltpu.CompilerParams(vmem_limit_bytes=6 * 2**20),
        cost_estimate=pl.CostEstimate(
            flops=2 * tokens * height * wide * 7,
            bytes_accessed=8 * 2**20,
            transcendentals=2 * tokens * width,
        ),
        name="gate_late",
    )(rank, *late, merged, total, square, magnitude, hidden, saved, lowrank_up)


def rest_kernel(factor, count, rank_ref, merged_ref, scaled_ref, latent_ref, both_ref, *refs):
    blocks, up_piece_ref, outs = refs[:count], refs[count], refs[count + 1 :]
    rank, sign = rank_ref[0], rank_ref[1]
    height = outs[0].shape[1]
    low, width = up_piece_ref.shape
    for offset, block, out in zip(REST_OUT, blocks, outs):
        rows = merged_ref[pl.ds(row_of(rank, offset, height, sign), height), :width]
        gradient_block(scaled_ref, rows, both_ref, block, out)
    both = dot(latent_ref[...], scaled_ref[...], 0, 0)
    up_piece_ref[...] = (both[:low] + both[low:]) * factor


def rest(factor, rank, merged, scaled, latent, both, blocks):
    tokens, width = scaled.shape
    height = blocks[0].shape[1]
    wide = merged.shape[1]
    count = len(REST_OUT)
    low = latent.shape[1] // 2
    return pl.pallas_call(
        functools.partial(rest_kernel, factor, count),
        in_specs=[SMEM] + [VMEM] * (4 + count),
        out_specs=[VMEM] * (count + 1),
        out_shape=[jax.ShapeDtypeStruct((low, width), jnp.float32)]
        + [jax.ShapeDtypeStruct((tokens + low, height), jnp.bfloat16)] * count,
        compiler_params=pltpu.CompilerParams(vmem_limit_bytes=6 * 2**20),
        cost_estimate=pl.CostEstimate(
            flops=2 * tokens * height * width * count,
            bytes_accessed=count * height * (wide + tokens) * 2,
            transcendentals=0,
        ),
        name="rest",
    )(rank, merged, scaled, latent, both, *blocks)


def payload_kernel(factor, tokens, rank_ref, up_ref, magnitude_ref, *refs):
    parts, (kept_ref, sent_ref) = refs[:4], refs[4:]
    low, width = up_ref.shape
    half = low // 2
    core = rank_ref[2]
    for out, upper in ((kept_ref, core), (sent_ref, 1 - core)):
        first = upper == 0
        here = pl.ds(pl.multiple_of(tokens + upper * half, half), half)
        down = sum(part[here, :].astype(jnp.float32) for part in parts) * factor
        out[:, :width] = jnp.where(first, up_ref[:half, :], up_ref[half:, :])
        out[:, width : width + down.shape[1]] = down
        out[:, width + down.shape[1] :] = jnp.zeros((half, LANES), jnp.float32)
        for row in range(width // LANES):
            out[row : row + 1, width + down.shape[1] :] = magnitude_ref[
                :, row * LANES : (row + 1) * LANES
            ]


def payload(factor, tokens, rank, up_piece, magnitude_piece, parts):
    low, width = up_piece.shape
    out = jax.ShapeDtypeStruct((low // 2, width + parts[0].shape[1] + LANES), jnp.float32)
    return pl.pallas_call(
        functools.partial(payload_kernel, factor, tokens),
        in_specs=[SMEM] + [VMEM] * 6,
        out_specs=[VMEM] * 2,
        out_shape=[out] * 2,
        compiler_params=pltpu.CompilerParams(vmem_limit_bytes=6 * 2**20),
        cost_estimate=pl.CostEstimate(flops=2**20, bytes_accessed=2**20, transcendentals=0),
        name="payload",
    )(rank, up_piece, magnitude_piece, *parts)


def f32(array):
    return array.astype(jnp.float32)


def narrow(*arrays):
    total = f32(arrays[0])
    for array in arrays[1:]:
        total = total + f32(array)
    return total.astype(jnp.bfloat16)


def sum_four(array, axis, bits):
    sent = lax.optimization_barrier(array.astype(jnp.bfloat16))
    one, two = bits
    near, far, both = (lax.ppermute(sent, axis, xor_perm(at)) for at in (one, two, one ^ two))
    return (f32(sent) + f32(near)) + (f32(far) + f32(both))


def pack(array):
    main, row = array[:, :-LANES], array[:16, -LANES:]
    high = lax.reduce_precision(row, 8, 7)
    return jnp.concatenate([main, jnp.concatenate([high, row - high], axis=0)], axis=1)


def unpack(array):
    main, row = array[:, :-LANES], array[:, -LANES:]
    row = row[:16] + row[16:]
    row = jnp.concatenate([row, jnp.zeros_like(row)], axis=0)
    return jnp.concatenate([main, row], axis=1)


def together(*arrays):
    return lax.optimization_barrier(arrays)


def per_device(
    stored_layer_input,
    saved_up_output,
    hidden_gradient,
    frozen_gate_weight,
    lowrank_down,
    lowrank_up,
    magnitude,
):
    own = stored_layer_input
    tokens, height = own.shape
    width = frozen_gate_weight.shape[1]
    low = lowrank_up.shape[0]
    factor = 1.0 / math.sqrt(tokens * lax.axis_size("dp"))
    core = lax.axis_index("dp") % 2
    rank = jnp.stack([lax.axis_index("tensor"), 1 - 2 * core, core]).astype(jnp.int32)
    rank, own = together(rank, own)

    operands = (frozen_gate_weight, jnp.transpose(lowrank_down), lowrank_up)
    head = merge(0, 2, operands, ())

    got = {(0, 0): own}
    token = own[:16, :128]

    def arrive(move, source, target, *more):
        nonlocal token
        block = move(got[source])
        token, got[target], *more = together(token, block, *more)
        return more

    head = arrive(up_ring, (0, 0), (0, -1), *head)
    arrive(down_ring, (0, 0), (0, 1))
    arrive(across, (0, 0), (1, 0))
    merged, square = merge(2, 6, operands, head)
    merged, square = arrive(up_ring, (0, -1), (0, -2), merged, square)
    arrive(down_ring, (0, 1), (0, 2))
    arrive(across, (0, -1), (1, -1))
    arrive(up_ring, (0, -2), (0, -3))
    arrive(down_ring, (0, 2), (0, 3))
    arrive(across, (0, 1), (1, 1))
    arrive(up_ring, (0, -3), (0, 4))
    arrive(down_ring, (1, 1), (1, 2))
    arrive(across, (0, -2), (1, -2))
    total = gate_early(rank, [got[offset] for offset in EARLY], merged)
    (total,) = arrive(up_ring, (1, -2), (1, -3), total)
    arrive(down_ring, (1, 2), (1, 3))
    arrive(across, (0, 4), (1, 4))
    *late, total = together(*[got[offset] for offset in LATE], total)

    up_output_gradient, scaled, both, latent, magnitude_piece, *first = gate_late(
        factor,
        rank,
        late,
        merged,
        total,
        square,
        magnitude.reshape(1, width),
        hidden_gradient,
        saved_up_output,
        lowrank_up,
    )
    lower, upper, far = down_ring(first[0]), up_ring(first[1]), across(first[2])
    up_piece, *others = rest(
        factor, rank, merged, scaled, latent, both, [got[offset] for offset in REST_OUT]
    )
    sums = {offset: [block] for offset, block in zip(REST_OUT, others)}

    def land(target, block):
        nonlocal up_piece
        up_piece, block = together(up_piece, block)
        sums[target].append(block)

    def send(move, source, target):
        land(target, move(narrow(*sums[source]) if len(sums[source]) > 1 else sums[source][0]))

    land((0, 4), far)
    land((1, 2), upper)
    land((1, -2), lower)
    send(down_ring, (0, 4), (0, -3))
    send(up_ring, (1, 2), (1, 1))
    send(across, (1, -2), (0, -2))
    send(up_ring, (0, 3), (0, 2))
    send(down_ring, (0, -3), (0, -2))
    send(across, (1, 1), (0, 1))
    send(across, (1, -1), (0, -1))
    send(up_ring, (0, 2), (0, 1))
    send(down_ring, (0, -2), (0, -1))
    send(across, (1, 0), (0, 0))
    send(up_ring, (0, 1), (0, 0))
    send(down_ring, (0, -1), (0, 0))
    last = together(*sums[0, 0])
    layer_input_gradient = narrow(*[one[:tokens] for one in last])

    kept, sent = payload(
        factor, tokens, rank, up_piece, magnitude_piece, last
    )
    pieces = kept + lax.ppermute(sent, "dp", xor_perm(1))
    pieces = unpack(sum_four(pack(pieces), "dp", (2, 4)))
    sent = lax.optimization_barrier(pack(pieces).astype(jnp.bfloat16))
    pieces = unpack(f32(sent) + f32(lax.ppermute(sent, "dp", xor_perm(8))))
    mine = pieces[:, :-LANES]
    other = lax.ppermute(mine, "dp", xor_perm(1))
    magnitude_gradient = pieces[: width // LANES, -LANES:].reshape(width)
    summed = jnp.where(
        core == 0,
        jnp.concatenate([mine, other], axis=0),
        jnp.concatenate([other, mine], axis=0),
    )
    return (
        layer_input_gradient,
        up_output_gradient,
        jnp.transpose(summed[:, width:]),
        summed[:, :width],
        magnitude_gradient,
    )


def solution(mesh):
    return jax.shard_map(
        per_device,
        mesh=mesh,
        in_specs=(
            P("dp", "tensor"),
            P("dp", "tensor"),
            P("dp", "tensor"),
            P(None, "tensor"),
            P(),
            P(None, "tensor"),
            P("tensor"),
        ),
        out_specs=(
            P("dp", "tensor"),
            P("dp", "tensor"),
            P("tensor", None),
            P(None, "tensor"),
            P("tensor"),
        ),
        check_vma=False,
    )
```

```python
import functools
import math

import jax
import jax.numpy as jnp
from jax import lax
from jax.experimental import pallas as pl
from jax.experimental.pallas import tpu as pltpu
from jax.sharding import PartitionSpec as P

EPSILON = 1e-06
RING = 8
PAIR = 2
MERGE_ROWS = 512
LANES = 128

EARLY = (
    (0, 0),
    (0, -1), (0, 1), (1, 0),
    (0, -2), (0, 2), (1, -1),
    (0, -3), (0, 3), (1, 1),
    (0, 4), (1, 2), (1, -2),
)
LATE = ((1, -3), (1, 3), (1, 4))
REST_OUT = (
    (0, 4), (1, 2), (1, -2), (0, -3), (0, 3), (1, 1), (0, -2), (0, 2), (1, -1),
    (0, -1), (0, 1), (1, 0), (0, 0),
)

VMEM = pl.BlockSpec(memory_space=pltpu.VMEM)
SMEM = pl.BlockSpec(memory_space=pltpu.SMEM)


def ring_perm(step):
    pairs = []
    for group in range(16):
        move = -step if group % 2 else step
        for pair in range(PAIR):
            for at in range(RING):
                source = (group * PAIR + pair) * RING + at
                pairs.append((source, source - at + (at + move) % RING))
    return pairs


def xor_perm(bits):
    return [(at, at ^ bits) for at in range(16)]


def up_ring(array):
    return lax.ppermute(array, ("dp", "tensor"), ring_perm(1))


def down_ring(array):
    return lax.ppermute(array, ("dp", "tensor"), ring_perm(-1))


def across(array):
    return lax.ppermute(array, "tensor", xor_perm(RING))


def dot(left, right, left_dim, right_dim):
    return lax.dot_general(
        left, right, (((left_dim,), (right_dim,)), ((), ())), preferred_element_type=jnp.float32
    )


def row_of(rank, offset, height, sign):
    pair, ring = offset
    ring = ring * sign
    own_pair, own_ring = rank // RING, rank % RING
    other = own_pair if pair == 0 else 1 - own_pair
    block = other * RING + (own_ring + ring + RING) % RING
    return pl.multiple_of(block * height, height)


def merge_rows(first, parts, weight_ref, down_ref, up_ref, merged_ref, square_ref):
    width = weight_ref.shape[1]

    @pl.loop(first, first + parts)
    def _(part):
        here = pl.ds(pl.multiple_of(part * MERGE_ROWS, MERGE_ROWS), MERGE_ROWS)
        down = down_ref[:, here]
        wide = weight_ref[here, :].astype(jnp.float32) + dot(down, up_ref[...], 0, 0)
        merged_ref[here, :width] = wide.astype(jnp.bfloat16)
        merged_ref[here, width:] = jnp.concatenate([down, jnp.zeros_like(down)], axis=0).T
        square_ref[...] += jnp.sum(wide * wide, axis=0, keepdims=True)


def merge_head_kernel(parts, weight_ref, down_ref, up_ref, merged_ref, square_ref):
    square_ref[...] = jnp.zeros_like(square_ref)
    merge_rows(0, parts, weight_ref, down_ref, up_ref, merged_ref, square_ref)


def merge_tail_kernel(
    first, parts, weight_ref, down_ref, up_ref, head_ref, head_square_ref, merged_ref, square_ref
):
    square_ref[...] = head_square_ref[...]
    merge_rows(first, parts, weight_ref, down_ref, up_ref, merged_ref, square_ref)


def merge(first, parts, operands, head):
    weight, down_t, _ = operands
    depth, width = weight.shape
    rank = down_t.shape[0]
    rows = parts * MERGE_ROWS
    if head:
        kernel, aliases = functools.partial(merge_tail_kernel, first, parts), {3: 0}
    else:
        kernel, aliases = functools.partial(merge_head_kernel, parts), {}
    return pl.pallas_call(
        kernel,
        in_specs=[VMEM] * (3 + len(head)),
        out_specs=[VMEM] * 2,
        out_shape=[
            jax.ShapeDtypeStruct((depth, width + 2 * rank), jnp.bfloat16),
            jax.ShapeDtypeStruct((1, width), jnp.float32),
        ],
        input_output_aliases=aliases,
        compiler_params=pltpu.CompilerParams(vmem_limit_bytes=6 * 2**20),
        cost_estimate=pl.CostEstimate(
            flops=2 * rows * width * rank, bytes_accessed=4 * rows * width, transcendentals=0
        ),
        name="merge_tail" if head else "merge_head",
    )(*operands, *head)


def split(array):
    high = array.astype(jnp.bfloat16)
    low = (array - high.astype(jnp.float32)).astype(jnp.bfloat16)
    return jnp.concatenate([high, low], axis=0)


def gradient_block(scaled_ref, rows, both_ref, block_ref, out_ref):
    tokens = scaled_ref.shape[0]
    low = both_ref.shape[0] // 2
    out_ref[:tokens, :] = dot(scaled_ref[...], rows, 1, 1).astype(jnp.bfloat16)
    down = dot(both_ref[...], block_ref[...], 1, 0)
    out_ref[tokens:, :] = (down[:low] + down[low:]).astype(jnp.bfloat16)


def gate_early_kernel(count, rank_ref, *refs):
    blocks, merged_ref, total_ref = refs[:count], refs[count], refs[count + 1]
    rank, sign = rank_ref[0], rank_ref[1]
    height = blocks[0].shape[1]
    for at, offset in enumerate(EARLY):
        rows = merged_ref[pl.ds(row_of(rank, offset, height, sign), height), :]
        part = dot(blocks[at][...], rows, 1, 0)
        if at == 0:
            total_ref[...] = part
        else:
            total_ref[...] += part


def gate_early(rank, blocks, merged):
    tokens, height = blocks[0].shape
    wide = merged.shape[1]
    count = len(blocks)
    return pl.pallas_call(
        functools.partial(gate_early_kernel, count),
        in_specs=[SMEM] + [VMEM] * (count + 1),
        out_specs=VMEM,
        out_shape=jax.ShapeDtypeStruct((tokens, wide), jnp.float32),
        compiler_params=pltpu.CompilerParams(vmem_limit_bytes=6 * 2**20),
        cost_estimate=pl.CostEstimate(
            flops=2 * tokens * height * wide * count,
            bytes_accessed=count * height * (wide + tokens) * 2 + tokens * wide * 4,
            transcendentals=0,
        ),
        name="gate_early",
    )(rank, *blocks, merged)


def gate_late_kernel(
    factor,
    rank_ref,
    late_a,
    late_b,
    late_c,
    merged_ref,
    total_ref,
    square_ref,
    magnitude_ref,
    hidden_ref,
    saved_ref,
    lowrank_up_ref,
    up_out_ref,
    scaled_ref,
    both_ref,
    latent_ref,
    magnitude_piece_ref,
    first_a,
    first_b,
    first_c,
):
    rank, sign = rank_ref[0], rank_ref[1]
    tokens, height = late_a.shape
    width = hidden_ref.shape[1]
    low = lowrank_up_ref.shape[0]
    norms = jnp.sqrt(square_ref[...] + EPSILON)
    scales = magnitude_ref[...] / norms
    tile = tokens
    starts = [row_of(rank, offset, height, sign) for offset in LATE]
    magnitude_piece_ref[...] = jnp.zeros_like(magnitude_piece_ref)

    @pl.loop(0, tokens // tile)
    def _(step):
        here = pl.ds(pl.multiple_of(step * tile, tile), tile)
        total = total_ref[here, :]
        for block, start in zip((late_a, late_b, late_c), starts):
            total += dot(block[here, :], merged_ref[pl.ds(start, height), :], 1, 0)
        gate_pre = total[:, :width]
        latent = total[:, width : width + low]
        gate_out = gate_pre * scales
        gate_sig = 1.0 / (1.0 + jnp.exp(-gate_out))
        cotangent = hidden_ref[here, :].astype(jnp.float32)
        up_out_ref[here, :] = (cotangent * gate_out * gate_sig).astype(jnp.bfloat16)
        gate_grad = (
            cotangent
            * saved_ref[here, :].astype(jnp.float32)
            * gate_sig
            * (1.0 + gate_out * (1.0 - gate_sig))
        )
        magnitude_piece_ref[...] += jnp.sum(gate_grad * gate_pre, axis=0, keepdims=True)
        scaled_ref[here, :] = (gate_grad * scales).astype(jnp.bfloat16)
        latent_high = latent.astype(jnp.bfloat16)
        latent_rest = (latent - latent_high.astype(jnp.float32)).astype(jnp.bfloat16)
        latent_ref[here, :] = jnp.concatenate([latent_high, latent_rest], axis=1)

    magnitude_piece_ref[...] = magnitude_piece_ref[...] / norms * factor
    both_ref[...] = split(dot(lowrank_up_ref[...], scaled_ref[...], 1, 1))
    for offset, block, out in zip(LATE, (late_a, late_b, late_c), (first_a, first_b, first_c)):
        rows = merged_ref[pl.ds(row_of(rank, offset, height, sign), height), :width]
        gradient_block(scaled_ref, rows, both_ref, block, out)


def gate_late(factor, rank, late, merged, total, square, magnitude, hidden, saved, lowrank_up):
    tokens, height = late[0].shape
    wide = merged.shape[1]
    width = hidden.shape[1]
    low = lowrank_up.shape[0]
    block = jax.ShapeDtypeStruct((tokens + low, height), jnp.bfloat16)
    return pl.pallas_call(
        functools.partial(gate_late_kernel, factor),
        in_specs=[SMEM] + [VMEM] * 10,
        out_specs=[VMEM] * 8,
        out_shape=[
            jax.ShapeDtypeStruct((tokens, width), jnp.bfloat16),
            jax.ShapeDtypeStruct((tokens, width), jnp.bfloat16),
            jax.ShapeDtypeStruct((2 * low, tokens), jnp.bfloat16),
            jax.ShapeDtypeStruct((tokens, 2 * low), jnp.bfloat16),
            jax.ShapeDtypeStruct((1, width), jnp.float32),
            block,
            block,
            block,
        ],
        compiler_params=pltpu.CompilerParams(vmem_limit_bytes=6 * 2**20),
        cost_estimate=pl.CostEstimate(
            flops=2 * tokens * height * wide * 7,
            bytes_accessed=8 * 2**20,
            transcendentals=2 * tokens * width,
        ),
        name="gate_late",
    )(rank, *late, merged, total, square, magnitude, hidden, saved, lowrank_up)


def rest_kernel(factor, count, rank_ref, merged_ref, scaled_ref, latent_ref, both_ref, *refs):
    blocks, up_piece_ref, outs = refs[:count], refs[count], refs[count + 1 :]
    rank, sign = rank_ref[0], rank_ref[1]
    height = outs[0].shape[1]
    low, width = up_piece_ref.shape
    for offset, block, out in zip(REST_OUT, blocks, outs):
        rows = merged_ref[pl.ds(row_of(rank, offset, height, sign), height), :width]
        gradient_block(scaled_ref, rows, both_ref, block, out)
    both = dot(latent_ref[...], scaled_ref[...], 0, 0)
    up_piece_ref[...] = (both[:low] + both[low:]) * factor


def rest(factor, rank, merged, scaled, latent, both, blocks):
    tokens, width = scaled.shape
    height = blocks[0].shape[1]
    wide = merged.shape[1]
    count = len(REST_OUT)
    low = latent.shape[1] // 2
    return pl.pallas_call(
        functools.partial(rest_kernel, factor, count),
        in_specs=[SMEM] + [VMEM] * (4 + count),
        out_specs=[VMEM] * (count + 1),
        out_shape=[jax.ShapeDtypeStruct((low, width), jnp.float32)]
        + [jax.ShapeDtypeStruct((tokens + low, height), jnp.bfloat16)] * count,
        compiler_params=pltpu.CompilerParams(vmem_limit_bytes=6 * 2**20),
        cost_estimate=pl.CostEstimate(
            flops=2 * tokens * height * width * count,
            bytes_accessed=count * height * (wide + tokens) * 2,
            transcendentals=0,
        ),
        name="rest",
    )(rank, merged, scaled, latent, both, *blocks)


def payload_kernel(factor, tokens, rank_ref, up_ref, magnitude_ref, *refs):
    parts, (kept_ref, sent_ref) = refs[:4], refs[4:]
    low, width = up_ref.shape
    half = low // 2
    core = rank_ref[2]
    for out, upper in ((kept_ref, core), (sent_ref, 1 - core)):
        first = upper == 0
        here = pl.ds(pl.multiple_of(tokens + upper * half, half), half)
        down = sum(part[here, :].astype(jnp.float32) for part in parts) * factor
        out[:, :width] = jnp.where(first, up_ref[:half, :], up_ref[half:, :])
        out[:, width : width + down.shape[1]] = down
        out[:, width + down.shape[1] :] = jnp.zeros((half, LANES), jnp.float32)
        for row in range(width // LANES):
            out[row : row + 1, width + down.shape[1] :] = magnitude_ref[
                :, row * LANES : (row + 1) * LANES
            ]


def payload(factor, tokens, rank, up_piece, magnitude_piece, parts):
    low, width = up_piece.shape
    out = jax.ShapeDtypeStruct((low // 2, width + parts[0].shape[1] + LANES), jnp.float32)
    return pl.pallas_call(
        functools.partial(payload_kernel, factor, tokens),
        in_specs=[SMEM] + [VMEM] * 6,
        out_specs=[VMEM] * 2,
        out_shape=[out] * 2,
        compiler_params=pltpu.CompilerParams(vmem_limit_bytes=6 * 2**20),
        cost_estimate=pl.CostEstimate(flops=2**20, bytes_accessed=2**20, transcendentals=0),
        name="payload",
    )(rank, up_piece, magnitude_piece, *parts)


def finish_kernel(rank_ref, mine_ref, other_ref, up_ref, down_ref):
    half, width = mine_ref.shape[0], up_ref.shape[1]
    first = rank_ref[2] == 0
    for at in range(2):
        here = slice(at * half, (at + 1) * half)
        rows = jnp.where(first == (at == 0), mine_ref[...], other_ref[...])
        up_ref[here, :] = rows[:, :width]
        down_ref[here, :] = rows[:, width:]


def finish(rank, mine, other, width):
    half, wide = mine.shape
    return pl.pallas_call(
        finish_kernel,
        in_specs=[SMEM] + [VMEM] * 2,
        out_specs=[VMEM] * 2,
        out_shape=[
            jax.ShapeDtypeStruct((2 * half, width), jnp.float32),
            jax.ShapeDtypeStruct((2 * half, wide - width), jnp.float32),
        ],
        compiler_params=pltpu.CompilerParams(vmem_limit_bytes=6 * 2**20),
        cost_estimate=pl.CostEstimate(flops=2**16, bytes_accessed=2**20, transcendentals=0),
        name="finish",
    )(rank, mine, other)


def f32(array):
    return array.astype(jnp.float32)


def narrow(*arrays):
    total = f32(arrays[0])
    for array in arrays[1:]:
        total = total + f32(array)
    return total.astype(jnp.bfloat16)


def sum_four(array, axis, bits):
    sent = lax.optimization_barrier(array.astype(jnp.bfloat16))
    one, two = bits
    near, far, both = (lax.ppermute(sent, axis, xor_perm(at)) for at in (one, two, one ^ two))
    return (f32(sent) + f32(near)) + (f32(far) + f32(both))


def pack(array):
    main, row = array[:, :-LANES], array[:16, -LANES:]
    high = lax.reduce_precision(row, 8, 7)
    return jnp.concatenate([main, jnp.concatenate([high, row - high], axis=0)], axis=1)


def unpack(array):
    main, row = array[:, :-LANES], array[:, -LANES:]
    row = row[:16] + row[16:]
    row = jnp.concatenate([row, jnp.zeros_like(row)], axis=0)
    return jnp.concatenate([main, row], axis=1)


def together(*arrays):
    return lax.optimization_barrier(arrays)


def per_device(
    stored_layer_input,
    saved_up_output,
    hidden_gradient,
    frozen_gate_weight,
    lowrank_down,
    lowrank_up,
    magnitude,
):
    own = stored_layer_input
    tokens, height = own.shape
    width = frozen_gate_weight.shape[1]
    low = lowrank_up.shape[0]
    factor = 1.0 / math.sqrt(tokens * lax.axis_size("dp"))
    core = lax.axis_index("dp") % 2
    rank = jnp.stack([lax.axis_index("tensor"), 1 - 2 * core, core]).astype(jnp.int32)
    rank, own = together(rank, own)

    operands = (frozen_gate_weight, jnp.transpose(lowrank_down), lowrank_up)
    head = merge(0, 1, operands, ())

    got = {(0, 0): own}
    token = own[:16, :128]

    def arrive(move, source, target, *more, after=None):
        nonlocal token
        block = got[source]
        if after is not None:
            block, _ = together(block, got[after])
        token, got[target], *more = together(token, move(block), *more)
        return more

    got[0, -1], got[0, 1], got[1, 0], *head = together(
        up_ring(own), down_ring(own), across(own), *head
    )
    merged, square = merge(1, 7, operands, head)
    merged, square = arrive(up_ring, (0, -1), (0, -2), merged, square)
    arrive(across, (0, 1), (1, 1))
    arrive(down_ring, (0, 1), (0, 2))
    arrive(up_ring, (0, -2), (0, -3))
    arrive(across, (0, -2), (1, -2))
    arrive(down_ring, (1, 1), (1, 2), after=(0, -2))
    arrive(up_ring, (0, -3), (0, 4))
    arrive(across, (0, -1), (1, -1), after=(0, -3))
    arrive(down_ring, (0, 2), (0, 3), after=(0, -3))
    total = gate_early(rank, [got[offset] for offset in EARLY], merged)
    (total,) = arrive(up_ring, (1, -2), (1, -3), total, after=(0, -3))
    arrive(down_ring, (1, 2), (1, 3), after=(0, -3))
    arrive(across, (0, 4), (1, 4))
    *late, total = together(*[got[offset] for offset in LATE], total)

    up_output_gradient, scaled, both, latent, magnitude_piece, *first = gate_late(
        factor,
        rank,
        late,
        merged,
        total,
        square,
        magnitude.reshape(1, width),
        hidden_gradient,
        saved_up_output,
        lowrank_up,
    )
    lower, upper, far = down_ring(first[0]), up_ring(first[1]), across(first[2])
    up_piece, *others = rest(
        factor, rank, merged, scaled, latent, both, [got[offset] for offset in REST_OUT]
    )
    far, lower, up_piece, *others = together(far, lower, up_piece, *others)
    sums = {offset: [block] for offset, block in zip(REST_OUT, others)}
    sums[0, 4].append(far)
    sums[1, -2].append(lower)

    def land(target, block):
        nonlocal up_piece
        up_piece, block = together(up_piece, block)
        sums[target].append(block)

    def send(move, source, target):
        land(target, move(narrow(*sums[source]) if len(sums[source]) > 1 else sums[source][0]))

    land((1, 2), upper)
    send(down_ring, (0, 4), (0, -3))
    send(up_ring, (1, 2), (1, 1))
    send(across, (1, -2), (0, -2))
    send(up_ring, (0, 3), (0, 2))
    send(down_ring, (0, -3), (0, -2))
    send(across, (1, 1), (0, 1))
    send(across, (1, -1), (0, -1))
    send(up_ring, (0, 2), (0, 1))
    send(down_ring, (0, -2), (0, -1))
    send(across, (1, 0), (0, 0))
    send(up_ring, (0, 1), (0, 0))
    send(down_ring, (0, -1), (0, 0))
    last = together(*sums[0, 0])
    layer_input_gradient = narrow(*[one[:tokens] for one in last])

    kept, sent = payload(
        factor, tokens, rank, up_piece, magnitude_piece, last
    )
    pieces = kept + lax.ppermute(sent, "dp", xor_perm(1))
    pieces = unpack(sum_four(pack(pieces), "dp", (2, 4)))
    sent = lax.optimization_barrier(pack(pieces).astype(jnp.bfloat16))
    pieces = unpack(f32(sent) + f32(lax.ppermute(sent, "dp", xor_perm(8))))
    mine = pieces[:, :-LANES]
    other = lax.ppermute(mine, "dp", xor_perm(1))
    lowrank_up_gradient, down_gradient = finish(rank, mine, other, width)
    magnitude_gradient = pieces[: width // LANES, -LANES:].reshape(width)
    return (
        layer_input_gradient,
        up_output_gradient,
        jnp.transpose(down_gradient),
        lowrank_up_gradient,
        magnitude_gradient,
    )


def solution(mesh):
    return jax.shard_map(
        per_device,
        mesh=mesh,
        in_specs=(
            P("dp", "tensor"),
            P("dp", "tensor"),
            P("dp", "tensor"),
            P(None, "tensor"),
            P(),
            P(None, "tensor"),
            P("tensor"),
        ),
        out_specs=(
            P("dp", "tensor"),
            P("dp", "tensor"),
            P("tensor", None),
            P(None, "tensor"),
            P("tensor"),
        ),
        check_vma=False,
    )
```

```python
import functools
import math

import jax
import jax.numpy as jnp
from jax import lax
from jax.experimental import pallas as pl
from jax.experimental.pallas import tpu as pltpu
from jax.sharding import PartitionSpec as P

EPSILON = 1e-06
RING = 8
PAIR = 2
MERGE_ROWS = 512
LANES = 128

GATE_FIRST = ((0, 0), (0, -1), (0, 1), (1, 0), (0, -2), (1, 1), (0, 2))
GATE_SECOND = ((0, -3), (1, -2), (1, 2), (0, 4), (1, -1), (0, 3))
GATE_THIRD = ((1, -3), (1, 3))
LATE = ((1, -3), (1, 3), (1, 4))
REST_OUT = (
    (0, 4), (1, 2), (1, -2), (0, -3), (0, 3), (1, 1), (0, -2), (0, 2), (1, -1),
    (0, -1), (0, 1), (1, 0), (0, 0),
)

VMEM = pl.BlockSpec(memory_space=pltpu.VMEM)
SMEM = pl.BlockSpec(memory_space=pltpu.SMEM)


def ring_perm(step):
    pairs = []
    for group in range(16):
        move = -step if group % 2 else step
        for pair in range(PAIR):
            for at in range(RING):
                source = (group * PAIR + pair) * RING + at
                pairs.append((source, source - at + (at + move) % RING))
    return pairs


def xor_perm(bits):
    return [(at, at ^ bits) for at in range(16)]


def up_ring(array):
    return lax.ppermute(array, ("dp", "tensor"), ring_perm(1))


def down_ring(array):
    return lax.ppermute(array, ("dp", "tensor"), ring_perm(-1))


def across(array):
    return lax.ppermute(array, "tensor", xor_perm(RING))


def dot(left, right, left_dim, right_dim):
    return lax.dot_general(
        left, right, (((left_dim,), (right_dim,)), ((), ())), preferred_element_type=jnp.float32
    )


def row_of(rank, offset, height, sign):
    pair, ring = offset
    ring = ring * sign
    own_pair, own_ring = rank // RING, rank % RING
    other = own_pair if pair == 0 else 1 - own_pair
    block = other * RING + (own_ring + ring + RING) % RING
    return pl.multiple_of(block * height, height)


def merge_rows(first, parts, weight_ref, down_ref, up_ref, merged_ref, square_ref):
    width = weight_ref.shape[1]

    @pl.loop(first, first + parts)
    def _(part):
        here = pl.ds(pl.multiple_of(part * MERGE_ROWS, MERGE_ROWS), MERGE_ROWS)
        down = down_ref[:, here]
        wide = weight_ref[here, :].astype(jnp.float32) + dot(down, up_ref[...], 0, 0)
        merged_ref[here, :width] = wide.astype(jnp.bfloat16)
        merged_ref[here, width:] = jnp.concatenate([down, jnp.zeros_like(down)], axis=0).T
        square_ref[...] += jnp.sum(wide * wide, axis=0, keepdims=True)


def merge_head_kernel(parts, weight_ref, down_ref, up_ref, merged_ref, square_ref):
    square_ref[...] = jnp.zeros_like(square_ref)
    merge_rows(0, parts, weight_ref, down_ref, up_ref, merged_ref, square_ref)


def merge_tail_kernel(
    first, parts, weight_ref, down_ref, up_ref, head_ref, head_square_ref, merged_ref, square_ref
):
    square_ref[...] = head_square_ref[...]
    merge_rows(first, parts, weight_ref, down_ref, up_ref, merged_ref, square_ref)


def merge(first, parts, operands, head):
    weight, down_t, _ = operands
    depth, width = weight.shape
    rank = down_t.shape[0]
    rows = parts * MERGE_ROWS
    if head:
        kernel, aliases = functools.partial(merge_tail_kernel, first, parts), {3: 0}
    else:
        kernel, aliases = functools.partial(merge_head_kernel, parts), {}
    return pl.pallas_call(
        kernel,
        in_specs=[VMEM] * (3 + len(head)),
        out_specs=[VMEM] * 2,
        out_shape=[
            jax.ShapeDtypeStruct((depth, width + 2 * rank), jnp.bfloat16),
            jax.ShapeDtypeStruct((1, width), jnp.float32),
        ],
        input_output_aliases=aliases,
        compiler_params=pltpu.CompilerParams(vmem_limit_bytes=6 * 2**20),
        cost_estimate=pl.CostEstimate(
            flops=2 * rows * width * rank, bytes_accessed=4 * rows * width, transcendentals=0
        ),
        name="merge_tail" if head else "merge_head",
    )(*operands, *head)


def split(array):
    high = array.astype(jnp.bfloat16)
    low = (array - high.astype(jnp.float32)).astype(jnp.bfloat16)
    return jnp.concatenate([high, low], axis=0)


def gradient_block(scaled_ref, rows, both_ref, block_ref, out_ref):
    tokens = scaled_ref.shape[0]
    low = both_ref.shape[0] // 2
    out_ref[:tokens, :] = dot(scaled_ref[...], rows, 1, 1).astype(jnp.bfloat16)
    down = dot(both_ref[...], block_ref[...], 1, 0)
    out_ref[tokens:, :] = (down[:low] + down[low:]).astype(jnp.bfloat16)


def gate_part_kernel(offsets, rank_ref, *refs):
    count = len(offsets)
    blocks, merged_ref, before, total_ref = refs[:count], refs[count], refs[count + 1 : -1], refs[-1]
    rank, sign = rank_ref[0], rank_ref[1]
    height = blocks[0].shape[1]
    for at, offset in enumerate(offsets):
        rows = merged_ref[pl.ds(row_of(rank, offset, height, sign), height), :]
        part = dot(blocks[at][...], rows, 1, 0)
        if at:
            total_ref[...] += part
        elif before:
            total_ref[...] = before[0][...] + part
        else:
            total_ref[...] = part


def gate_part(offsets, rank, blocks, merged, before=()):
    tokens, height = blocks[0].shape
    wide = merged.shape[1]
    count = len(blocks)
    return pl.pallas_call(
        functools.partial(gate_part_kernel, offsets),
        in_specs=[SMEM] + [VMEM] * (count + 1 + len(before)),
        out_specs=VMEM,
        out_shape=jax.ShapeDtypeStruct((tokens, wide), jnp.float32),
        input_output_aliases={count + 2: 0} if before else {},
        compiler_params=pltpu.CompilerParams(vmem_limit_bytes=6 * 2**20),
        cost_estimate=pl.CostEstimate(
            flops=2 * tokens * height * wide * count,
            bytes_accessed=count * height * (wide + tokens) * 2 + tokens * wide * 4,
            transcendentals=0,
        ),
        name="gate_part",
    )(rank, *blocks, merged, *before)


def gate_late_kernel(
    factor,
    rank_ref,
    late_a,
    late_b,
    late_c,
    merged_ref,
    total_ref,
    square_ref,
    magnitude_ref,
    hidden_ref,
    saved_ref,
    lowrank_up_ref,
    up_out_ref,
    scaled_ref,
    both_ref,
    latent_ref,
    magnitude_piece_ref,
    first_a,
    first_b,
    first_c,
):
    rank, sign = rank_ref[0], rank_ref[1]
    tokens, height = late_a.shape
    width = hidden_ref.shape[1]
    low = lowrank_up_ref.shape[0]
    norms = jnp.sqrt(square_ref[...] + EPSILON)
    scales = magnitude_ref[...] / norms
    tile = tokens
    start = row_of(rank, LATE[-1], height, sign)
    magnitude_piece_ref[...] = jnp.zeros_like(magnitude_piece_ref)

    @pl.loop(0, tokens // tile)
    def _(step):
        here = pl.ds(pl.multiple_of(step * tile, tile), tile)
        total = total_ref[here, :]
        total += dot(late_c[here, :], merged_ref[pl.ds(start, height), :], 1, 0)
        gate_pre = total[:, :width]
        latent = total[:, width : width + low]
        gate_out = gate_pre * scales
        gate_sig = 1.0 / (1.0 + jnp.exp(-gate_out))
        cotangent = hidden_ref[here, :].astype(jnp.float32)
        up_out_ref[here, :] = (cotangent * gate_out * gate_sig).astype(jnp.bfloat16)
        gate_grad = (
            cotangent
            * saved_ref[here, :].astype(jnp.float32)
            * gate_sig
            * (1.0 + gate_out * (1.0 - gate_sig))
        )
        magnitude_piece_ref[...] += jnp.sum(gate_grad * gate_pre, axis=0, keepdims=True)
        scaled_ref[here, :] = (gate_grad * scales).astype(jnp.bfloat16)
        latent_high = latent.astype(jnp.bfloat16)
        latent_rest = (latent - latent_high.astype(jnp.float32)).astype(jnp.bfloat16)
        latent_ref[here, :] = jnp.concatenate([latent_high, latent_rest], axis=1)

    magnitude_piece_ref[...] = magnitude_piece_ref[...] / norms * factor
    both_ref[...] = split(dot(lowrank_up_ref[...], scaled_ref[...], 1, 1))
    for offset, block, out in zip(LATE, (late_a, late_b, late_c), (first_a, first_b, first_c)):
        rows = merged_ref[pl.ds(row_of(rank, offset, height, sign), height), :width]
        gradient_block(scaled_ref, rows, both_ref, block, out)


def gate_late(factor, rank, late, merged, total, square, magnitude, hidden, saved, lowrank_up):
    tokens, height = late[0].shape
    wide = merged.shape[1]
    width = hidden.shape[1]
    low = lowrank_up.shape[0]
    block = jax.ShapeDtypeStruct((tokens + low, height), jnp.bfloat16)
    return pl.pallas_call(
        functools.partial(gate_late_kernel, factor),
        in_specs=[SMEM] + [VMEM] * 10,
        out_specs=[VMEM] * 8,
        out_shape=[
            jax.ShapeDtypeStruct((tokens, width), jnp.bfloat16),
            jax.ShapeDtypeStruct((tokens, width), jnp.bfloat16),
            jax.ShapeDtypeStruct((2 * low, tokens), jnp.bfloat16),
            jax.ShapeDtypeStruct((tokens, 2 * low), jnp.bfloat16),
            jax.ShapeDtypeStruct((1, width), jnp.float32),
            block,
            block,
            block,
        ],
        compiler_params=pltpu.CompilerParams(vmem_limit_bytes=6 * 2**20),
        cost_estimate=pl.CostEstimate(
            flops=2 * tokens * height * wide * 7,
            bytes_accessed=8 * 2**20,
            transcendentals=2 * tokens * width,
        ),
        name="gate_late",
    )(rank, *late, merged, total, square, magnitude, hidden, saved, lowrank_up)


def rest_kernel(factor, count, rank_ref, merged_ref, scaled_ref, latent_ref, both_ref, *refs):
    blocks, up_piece_ref, outs = refs[:count], refs[count], refs[count + 1 :]
    rank, sign = rank_ref[0], rank_ref[1]
    height = outs[0].shape[1]
    low, width = up_piece_ref.shape
    for offset, block, out in zip(REST_OUT, blocks, outs):
        rows = merged_ref[pl.ds(row_of(rank, offset, height, sign), height), :width]
        gradient_block(scaled_ref, rows, both_ref, block, out)
    both = dot(latent_ref[...], scaled_ref[...], 0, 0)
    up_piece_ref[...] = (both[:low] + both[low:]) * factor


def rest(factor, rank, merged, scaled, latent, both, blocks):
    tokens, width = scaled.shape
    height = blocks[0].shape[1]
    wide = merged.shape[1]
    count = len(REST_OUT)
    low = latent.shape[1] // 2
    return pl.pallas_call(
        functools.partial(rest_kernel, factor, count),
        in_specs=[SMEM] + [VMEM] * (4 + count),
        out_specs=[VMEM] * (count + 1),
        out_shape=[jax.ShapeDtypeStruct((low, width), jnp.float32)]
        + [jax.ShapeDtypeStruct((tokens + low, height), jnp.bfloat16)] * count,
        compiler_params=pltpu.CompilerParams(vmem_limit_bytes=6 * 2**20),
        cost_estimate=pl.CostEstimate(
            flops=2 * tokens * height * width * count,
            bytes_accessed=count * height * (wide + tokens) * 2,
            transcendentals=0,
        ),
        name="rest",
    )(rank, merged, scaled, latent, both, *blocks)


def payload_kernel(factor, tokens, rank_ref, up_ref, magnitude_ref, *refs):
    parts, (kept_ref, sent_ref) = refs[:4], refs[4:]
    low, width = up_ref.shape
    half = low // 2
    core = rank_ref[2]
    for out, upper in ((kept_ref, core), (sent_ref, 1 - core)):
        first = upper == 0
        here = pl.ds(pl.multiple_of(tokens + upper * half, half), half)
        down = sum(part[here, :].astype(jnp.float32) for part in parts) * factor
        out[:, :width] = jnp.where(first, up_ref[:half, :], up_ref[half:, :])
        out[:, width : width + down.shape[1]] = down
        out[:, width + down.shape[1] :] = jnp.zeros((half, LANES), jnp.float32)
        for row in range(width // LANES):
            out[row : row + 1, width + down.shape[1] :] = magnitude_ref[
                :, row * LANES : (row + 1) * LANES
            ]


def payload(factor, tokens, rank, up_piece, magnitude_piece, parts):
    low, width = up_piece.shape
    out = jax.ShapeDtypeStruct((low // 2, width + parts[0].shape[1] + LANES), jnp.float32)
    return pl.pallas_call(
        functools.partial(payload_kernel, factor, tokens),
        in_specs=[SMEM] + [VMEM] * 6,
        out_specs=[VMEM] * 2,
        out_shape=[out] * 2,
        compiler_params=pltpu.CompilerParams(vmem_limit_bytes=6 * 2**20),
        cost_estimate=pl.CostEstimate(flops=2**20, bytes_accessed=2**20, transcendentals=0),
        name="payload",
    )(rank, up_piece, magnitude_piece, *parts)


def finish_kernel(rank_ref, mine_ref, other_ref, up_ref, down_ref, magnitude_ref):
    half, width = mine_ref.shape[0], up_ref.shape[1]
    core = rank_ref[2]
    for ref, upper in ((mine_ref, core), (other_ref, 1 - core)):
        here = pl.ds(pl.multiple_of(upper * half, half), half)
        up_ref[here, :] = ref[:, :width]
        down_ref[here, :] = ref[:, width : width + down_ref.shape[1]]
    for row in range(width // LANES):
        magnitude_ref[pl.ds(row * LANES, LANES)] = mine_ref[row, -LANES:]


def finish(rank, mine, other, width):
    half, wide = other.shape
    return pl.pallas_call(
        finish_kernel,
        in_specs=[SMEM] + [VMEM] * 2,
        out_specs=[VMEM] * 3,
        out_shape=[
            jax.ShapeDtypeStruct((2 * half, width), jnp.float32),
            jax.ShapeDtypeStruct((2 * half, wide - width), jnp.float32),
            jax.ShapeDtypeStruct((width,), jnp.float32),
        ],
        compiler_params=pltpu.CompilerParams(vmem_limit_bytes=6 * 2**20),
        cost_estimate=pl.CostEstimate(flops=2**16, bytes_accessed=2**20, transcendentals=0),
        name="finish",
    )(rank, mine, other)


def f32(array):
    return array.astype(jnp.float32)


def narrow(*arrays):
    total = f32(arrays[0])
    for array in arrays[1:]:
        total = total + f32(array)
    return total.astype(jnp.bfloat16)


def sum_four(array, axis, bits):
    sent = lax.optimization_barrier(array.astype(jnp.bfloat16))
    one, two = bits
    near, far, both = (lax.ppermute(sent, axis, xor_perm(at)) for at in (one, two, one ^ two))
    return (f32(sent) + f32(near)) + (f32(far) + f32(both))


def pack(array):
    main, row = array[:, :-LANES], array[:16, -LANES:]
    high = lax.reduce_precision(row, 8, 7)
    return jnp.concatenate([main, jnp.concatenate([high, row - high], axis=0)], axis=1)


def unpack(array):
    main, row = array[:, :-LANES], array[:, -LANES:]
    row = row[:16] + row[16:]
    row = jnp.concatenate([row, jnp.zeros_like(row)], axis=0)
    return jnp.concatenate([main, row], axis=1)


def together(*arrays):
    return lax.optimization_barrier(arrays)


def per_device(
    stored_layer_input,
    saved_up_output,
    hidden_gradient,
    frozen_gate_weight,
    lowrank_down,
    lowrank_up,
    magnitude,
):
    own = stored_layer_input
    tokens, height = own.shape
    width = frozen_gate_weight.shape[1]
    low = lowrank_up.shape[0]
    factor = 1.0 / math.sqrt(tokens * lax.axis_size("dp"))
    core = lax.axis_index("dp") % 2
    rank = jnp.stack([lax.axis_index("tensor"), 1 - 2 * core, core]).astype(jnp.int32)
    rank, own = together(rank, own)

    operands = (frozen_gate_weight, jnp.transpose(lowrank_down), lowrank_up)
    head = merge(0, 1, operands, ())

    got = {(0, 0): own}
    token = own[:16, :128]

    def arrive(move, source, target, *more, after=None):
        nonlocal token
        block = got[source]
        if after is not None:
            block, _ = together(block, got[after])
        token, got[target], *more = together(token, move(block), *more)
        return more

    got[0, -1], got[0, 1], got[1, 0], *head = together(
        up_ring(own), down_ring(own), across(own), *head
    )
    merged, square = merge(1, 7, operands, head)
    merged, square = arrive(up_ring, (0, -1), (0, -2), merged, square)
    arrive(across, (0, 1), (1, 1))
    arrive(down_ring, (0, 1), (0, 2))
    total = gate_part(GATE_FIRST, rank, [got[offset] for offset in GATE_FIRST], merged)
    (total,) = arrive(up_ring, (0, -2), (0, -3), total)
    arrive(across, (0, -2), (1, -2))
    arrive(down_ring, (1, 1), (1, 2), after=(0, -2))
    arrive(up_ring, (0, -3), (0, 4))
    arrive(across, (0, -1), (1, -1), after=(0, -3))
    arrive(down_ring, (0, 2), (0, 3), after=(0, -3))
    total = gate_part(
        GATE_SECOND, rank, [got[offset] for offset in GATE_SECOND], merged, (total,)
    )
    (total,) = arrive(up_ring, (1, -2), (1, -3), total, after=(0, -3))
    arrive(down_ring, (1, 2), (1, 3), after=(0, -3))
    total = gate_part(GATE_THIRD, rank, [got[offset] for offset in GATE_THIRD], merged, (total,))
    arrive(across, (0, 4), (1, 4))
    *late, total = together(*[got[offset] for offset in LATE], total)

    up_output_gradient, scaled, both, latent, magnitude_piece, *first = gate_late(
        factor,
        rank,
        late,
        merged,
        total,
        square,
        magnitude.reshape(1, width),
        hidden_gradient,
        saved_up_output,
        lowrank_up,
    )
    lower, upper, far = down_ring(first[0]), up_ring(first[1]), across(first[2])
    up_piece, *others = rest(
        factor, rank, merged, scaled, latent, both, [got[offset] for offset in REST_OUT]
    )
    far, lower, up_piece, *others = together(far, lower, up_piece, *others)
    sums = {offset: [block] for offset, block in zip(REST_OUT, others)}
    sums[0, 4].append(far)
    sums[1, -2].append(lower)

    def land(target, block):
        nonlocal up_piece
        up_piece, block = together(up_piece, block)
        sums[target].append(block)

    def send(move, source, target):
        land(target, move(narrow(*sums[source]) if len(sums[source]) > 1 else sums[source][0]))

    land((1, 2), upper)
    send(down_ring, (0, 4), (0, -3))
    send(up_ring, (1, 2), (1, 1))
    send(across, (1, -2), (0, -2))
    send(up_ring, (0, 3), (0, 2))
    send(down_ring, (0, -3), (0, -2))
    send(across, (1, 1), (0, 1))
    send(across, (1, -1), (0, -1))
    send(up_ring, (0, 2), (0, 1))
    send(down_ring, (0, -2), (0, -1))
    send(across, (1, 0), (0, 0))
    send(up_ring, (0, 1), (0, 0))
    send(down_ring, (0, -1), (0, 0))
    last = together(*sums[0, 0])
    layer_input_gradient = narrow(*[one[:tokens] for one in last])

    kept, sent = payload(
        factor, tokens, rank, up_piece, magnitude_piece, last
    )
    pieces = kept + lax.ppermute(sent, "dp", xor_perm(1))
    pieces = unpack(sum_four(pack(pieces), "dp", (2, 4)))
    sent = lax.optimization_barrier(pack(pieces).astype(jnp.bfloat16))
    pieces = unpack(f32(sent) + f32(lax.ppermute(sent, "dp", xor_perm(8))))
    other = lax.ppermute(pieces[:, :-LANES], "dp", xor_perm(1))
    lowrank_up_gradient, down_gradient, magnitude_gradient = finish(rank, pieces, other, width)
    return (
        layer_input_gradient,
        up_output_gradient,
        jnp.transpose(down_gradient),
        lowrank_up_gradient,
        magnitude_gradient,
    )


def solution(mesh):
    return jax.shard_map(
        per_device,
        mesh=mesh,
        in_specs=(
            P("dp", "tensor"),
            P("dp", "tensor"),
            P("dp", "tensor"),
            P(None, "tensor"),
            P(),
            P(None, "tensor"),
            P("tensor"),
        ),
        out_specs=(
            P("dp", "tensor"),
            P("dp", "tensor"),
            P("tensor", None),
            P(None, "tensor"),
            P("tensor"),
        ),
        check_vma=False,
    )
```

```python
import functools
import math

import jax
import jax.numpy as jnp
from jax import lax
from jax.experimental import pallas as pl
from jax.experimental.pallas import tpu as pltpu
from jax.sharding import PartitionSpec as P

EPSILON = 1e-06
RING = 8
PAIR = 2
MERGE_ROWS = 512
LANES = 128

GATE_FIRST = ((0, 0), (0, -1), (0, 1), (1, 0), (0, -2), (1, 1), (0, 2))
GATE_SECOND = ((0, -3), (1, -2), (1, 2), (0, 4), (1, -1), (0, 3))
GATE_THIRD = ((1, -3), (1, 3))
LATE = ((1, -3), (1, 3), (1, 4))
REST_OUT = (
    (0, 4), (1, 2), (1, -2), (0, -3), (0, 3), (1, 1), (0, -2), (0, 2), (1, -1),
    (0, -1), (0, 1), (1, 0), (0, 0),
)

VMEM = pl.BlockSpec(memory_space=pltpu.VMEM)
SMEM = pl.BlockSpec(memory_space=pltpu.SMEM)


def ring_perm(step):
    pairs = []
    for group in range(16):
        move = -step if group % 2 else step
        for pair in range(PAIR):
            for at in range(RING):
                source = (group * PAIR + pair) * RING + at
                pairs.append((source, source - at + (at + move) % RING))
    return pairs


def xor_perm(bits):
    return [(at, at ^ bits) for at in range(16)]


def up_ring(array):
    return lax.ppermute(array, ("dp", "tensor"), ring_perm(1))


def down_ring(array):
    return lax.ppermute(array, ("dp", "tensor"), ring_perm(-1))


def across(array):
    return lax.ppermute(array, "tensor", xor_perm(RING))


def dot(left, right, left_dim, right_dim):
    return lax.dot_general(
        left, right, (((left_dim,), (right_dim,)), ((), ())), preferred_element_type=jnp.float32
    )


def place():
    return lax.axis_index("tensor"), 1 - 2 * (lax.axis_index("dp") % 2)


def row_of(rank, offset, height, sign):
    pair, ring = offset
    ring = ring * sign
    own_pair, own_ring = rank // RING, rank % RING
    other = own_pair if pair == 0 else 1 - own_pair
    block = other * RING + (own_ring + ring + RING) % RING
    return pl.multiple_of(block * height, height)


def merge_rows(first, parts, weight_ref, down_ref, up_ref, merged_ref, square_ref):
    width = weight_ref.shape[1]

    @pl.loop(first, first + parts)
    def _(part):
        here = pl.ds(pl.multiple_of(part * MERGE_ROWS, MERGE_ROWS), MERGE_ROWS)
        down = down_ref[:, here]
        wide = weight_ref[here, :].astype(jnp.float32) + dot(down, up_ref[...], 0, 0)
        merged_ref[here, :width] = wide.astype(jnp.bfloat16)
        merged_ref[here, width:] = jnp.concatenate([down, jnp.zeros_like(down)], axis=0).T
        square_ref[...] += jnp.sum(wide * wide, axis=0, keepdims=True)


def merge_head_kernel(parts, weight_ref, down_ref, up_ref, merged_ref, square_ref):
    square_ref[...] = jnp.zeros_like(square_ref)
    merge_rows(0, parts, weight_ref, down_ref, up_ref, merged_ref, square_ref)


def merge_tail_kernel(
    first, parts, weight_ref, down_ref, up_ref, head_ref, head_square_ref, merged_ref, square_ref
):
    square_ref[...] = head_square_ref[...]
    merge_rows(first, parts, weight_ref, down_ref, up_ref, merged_ref, square_ref)


def merge(first, parts, operands, head):
    weight, down_t, _ = operands
    depth, width = weight.shape
    rank = down_t.shape[0]
    rows = parts * MERGE_ROWS
    if head:
        kernel, aliases = functools.partial(merge_tail_kernel, first, parts), {3: 0}
    else:
        kernel, aliases = functools.partial(merge_head_kernel, parts), {}
    return pl.pallas_call(
        kernel,
        in_specs=[VMEM] * (3 + len(head)),
        out_specs=[VMEM] * 2,
        out_shape=[
            jax.ShapeDtypeStruct((depth, width + 2 * rank), jnp.bfloat16),
            jax.ShapeDtypeStruct((1, width), jnp.float32),
        ],
        input_output_aliases=aliases,
        compiler_params=pltpu.CompilerParams(vmem_limit_bytes=6 * 2**20),
        cost_estimate=pl.CostEstimate(
            flops=2 * rows * width * rank, bytes_accessed=4 * rows * width, transcendentals=0
        ),
        name="merge_tail" if head else "merge_head",
    )(*operands, *head)


def split(array):
    high = array.astype(jnp.bfloat16)
    low = (array - high.astype(jnp.float32)).astype(jnp.bfloat16)
    return jnp.concatenate([high, low], axis=0)


def gradient_block(scaled_ref, rows, both_ref, block_ref, out_ref):
    tokens = scaled_ref.shape[0]
    low = both_ref.shape[0] // 2
    out_ref[:tokens, :] = dot(scaled_ref[...], rows, 1, 1).astype(jnp.bfloat16)
    down = dot(both_ref[...], block_ref[...], 1, 0)
    out_ref[tokens:, :] = (down[:low] + down[low:]).astype(jnp.bfloat16)


def gate_part_kernel(offsets, *refs):
    count = len(offsets)
    blocks, merged_ref, before, total_ref = refs[:count], refs[count], refs[count + 1 : -1], refs[-1]
    rank, sign = place()
    height = blocks[0].shape[1]
    for at, offset in enumerate(offsets):
        rows = merged_ref[pl.ds(row_of(rank, offset, height, sign), height), :]
        part = dot(blocks[at][...], rows, 1, 0)
        if at:
            total_ref[...] += part
        elif before:
            total_ref[...] = before[0][...] + part
        else:
            total_ref[...] = part


def gate_part(offsets, rank, blocks, merged, before=()):
    tokens, height = blocks[0].shape
    wide = merged.shape[1]
    count = len(blocks)
    return pl.pallas_call(
        functools.partial(gate_part_kernel, offsets),
        in_specs=[VMEM] * (count + 1 + len(before)),
        out_specs=VMEM,
        out_shape=jax.ShapeDtypeStruct((tokens, wide), jnp.float32),
        input_output_aliases={count + 1: 0} if before else {},
        compiler_params=pltpu.CompilerParams(vmem_limit_bytes=6 * 2**20),
        cost_estimate=pl.CostEstimate(
            flops=2 * tokens * height * wide * count,
            bytes_accessed=count * height * (wide + tokens) * 2 + tokens * wide * 4,
            transcendentals=0,
        ),
        name="gate_part",
    )(*blocks, merged, *before)


def gate_late_kernel(
    factor,
    late_a,
    late_b,
    late_c,
    merged_ref,
    total_ref,
    square_ref,
    magnitude_ref,
    hidden_ref,
    saved_ref,
    lowrank_up_ref,
    up_out_ref,
    scaled_ref,
    both_ref,
    latent_ref,
    magnitude_piece_ref,
    first_a,
    first_b,
    first_c,
):
    rank, sign = place()
    tokens, height = late_a.shape
    width = hidden_ref.shape[1]
    low = lowrank_up_ref.shape[0]
    norms = jnp.sqrt(square_ref[...] + EPSILON)
    scales = magnitude_ref[...] / norms
    tile = tokens
    start = row_of(rank, LATE[-1], height, sign)
    magnitude_piece_ref[...] = jnp.zeros_like(magnitude_piece_ref)

    @pl.loop(0, tokens // tile)
    def _(step):
        here = pl.ds(pl.multiple_of(step * tile, tile), tile)
        total = total_ref[here, :]
        total += dot(late_c[here, :], merged_ref[pl.ds(start, height), :], 1, 0)
        gate_pre = total[:, :width]
        latent = total[:, width : width + low]
        gate_out = gate_pre * scales
        gate_sig = 1.0 / (1.0 + jnp.exp(-gate_out))
        cotangent = hidden_ref[here, :].astype(jnp.float32)
        up_out_ref[here, :] = (cotangent * gate_out * gate_sig).astype(jnp.bfloat16)
        gate_grad = (
            cotangent
            * saved_ref[here, :].astype(jnp.float32)
            * gate_sig
            * (1.0 + gate_out * (1.0 - gate_sig))
        )
        magnitude_piece_ref[...] += jnp.sum(gate_grad * gate_pre, axis=0, keepdims=True)
        scaled_ref[here, :] = (gate_grad * scales).astype(jnp.bfloat16)
        latent_high = latent.astype(jnp.bfloat16)
        latent_rest = (latent - latent_high.astype(jnp.float32)).astype(jnp.bfloat16)
        latent_ref[here, :] = jnp.concatenate([latent_high, latent_rest], axis=1)

    magnitude_piece_ref[...] = magnitude_piece_ref[...] / norms * factor
    both_ref[...] = split(dot(lowrank_up_ref[...], scaled_ref[...], 1, 1))
    for offset, block, out in zip(LATE, (late_a, late_b, late_c), (first_a, first_b, first_c)):
        rows = merged_ref[pl.ds(row_of(rank, offset, height, sign), height), :width]
        gradient_block(scaled_ref, rows, both_ref, block, out)


def gate_late(factor, rank, late, merged, total, square, magnitude, hidden, saved, lowrank_up):
    tokens, height = late[0].shape
    wide = merged.shape[1]
    width = hidden.shape[1]
    low = lowrank_up.shape[0]
    block = jax.ShapeDtypeStruct((tokens + low, height), jnp.bfloat16)
    return pl.pallas_call(
        functools.partial(gate_late_kernel, factor),
        in_specs=[VMEM] * 10,
        out_specs=[VMEM] * 8,
        out_shape=[
            jax.ShapeDtypeStruct((tokens, width), jnp.bfloat16),
            jax.ShapeDtypeStruct((tokens, width), jnp.bfloat16),
            jax.ShapeDtypeStruct((2 * low, tokens), jnp.bfloat16),
            jax.ShapeDtypeStruct((tokens, 2 * low), jnp.bfloat16),
            jax.ShapeDtypeStruct((1, width), jnp.float32),
            block,
            block,
            block,
        ],
        compiler_params=pltpu.CompilerParams(vmem_limit_bytes=6 * 2**20),
        cost_estimate=pl.CostEstimate(
            flops=2 * tokens * height * wide * 7,
            bytes_accessed=8 * 2**20,
            transcendentals=2 * tokens * width,
        ),
        name="gate_late",
    )(*late, merged, total, square, magnitude, hidden, saved, lowrank_up)


def rest_kernel(factor, count, merged_ref, scaled_ref, latent_ref, both_ref, *refs):
    blocks, up_piece_ref, outs = refs[:count], refs[count], refs[count + 1 :]
    rank, sign = place()
    height = outs[0].shape[1]
    low, width = up_piece_ref.shape
    for offset, block, out in zip(REST_OUT, blocks, outs):
        rows = merged_ref[pl.ds(row_of(rank, offset, height, sign), height), :width]
        gradient_block(scaled_ref, rows, both_ref, block, out)
    both = dot(latent_ref[...], scaled_ref[...], 0, 0)
    up_piece_ref[...] = (both[:low] + both[low:]) * factor


def rest(factor, rank, merged, scaled, latent, both, blocks):
    tokens, width = scaled.shape
    height = blocks[0].shape[1]
    wide = merged.shape[1]
    count = len(REST_OUT)
    low = latent.shape[1] // 2
    return pl.pallas_call(
        functools.partial(rest_kernel, factor, count),
        in_specs=[VMEM] * (4 + count),
        out_specs=[VMEM] * (count + 1),
        out_shape=[jax.ShapeDtypeStruct((low, width), jnp.float32)]
        + [jax.ShapeDtypeStruct((tokens + low, height), jnp.bfloat16)] * count,
        compiler_params=pltpu.CompilerParams(vmem_limit_bytes=6 * 2**20),
        cost_estimate=pl.CostEstimate(
            flops=2 * tokens * height * width * count,
            bytes_accessed=count * height * (wide + tokens) * 2,
            transcendentals=0,
        ),
        name="rest",
    )(merged, scaled, latent, both, *blocks)


def payload_kernel(factor, tokens, up_ref, magnitude_ref, *refs):
    parts, (kept_ref, sent_ref) = refs[:4], refs[4:]
    low, width = up_ref.shape
    half = low // 2
    core = lax.axis_index("dp") % 2
    for out, upper in ((kept_ref, core), (sent_ref, 1 - core)):
        first = upper == 0
        here = pl.ds(pl.multiple_of(tokens + upper * half, half), half)
        down = sum(part[here, :].astype(jnp.float32) for part in parts) * factor
        out[:, :width] = jnp.where(first, up_ref[:half, :], up_ref[half:, :])
        out[:, width : width + down.shape[1]] = down
        out[:, width + down.shape[1] :] = jnp.zeros((half, LANES), jnp.float32)
        for row in range(width // LANES):
            out[row : row + 1, width + down.shape[1] :] = magnitude_ref[
                :, row * LANES : (row + 1) * LANES
            ]


def payload(factor, tokens, rank, up_piece, magnitude_piece, parts):
    low, width = up_piece.shape
    out = jax.ShapeDtypeStruct((low // 2, width + parts[0].shape[1] + LANES), jnp.float32)
    return pl.pallas_call(
        functools.partial(payload_kernel, factor, tokens),
        in_specs=[VMEM] * 6,
        out_specs=[VMEM] * 2,
        out_shape=[out] * 2,
        compiler_params=pltpu.CompilerParams(vmem_limit_bytes=6 * 2**20),
        cost_estimate=pl.CostEstimate(flops=2**20, bytes_accessed=2**20, transcendentals=0),
        name="payload",
    )(up_piece, magnitude_piece, *parts)


def finish_kernel(mine_ref, other_ref, up_ref, down_ref, magnitude_ref):
    half, width = mine_ref.shape[0], up_ref.shape[1]
    core = lax.axis_index("dp") % 2
    for ref, upper in ((mine_ref, core), (other_ref, 1 - core)):
        here = pl.ds(pl.multiple_of(upper * half, half), half)
        up_ref[here, :] = ref[:, :width]
        down_ref[here, :] = ref[:, width : width + down_ref.shape[1]]
    for row in range(width // LANES):
        magnitude_ref[pl.ds(row * LANES, LANES)] = mine_ref[row, -LANES:]


def finish(rank, mine, other, width):
    half, wide = other.shape
    return pl.pallas_call(
        finish_kernel,
        in_specs=[VMEM] * 2,
        out_specs=[VMEM] * 3,
        out_shape=[
            jax.ShapeDtypeStruct((2 * half, width), jnp.float32),
            jax.ShapeDtypeStruct((2 * half, wide - width), jnp.float32),
            jax.ShapeDtypeStruct((width,), jnp.float32),
        ],
        compiler_params=pltpu.CompilerParams(vmem_limit_bytes=6 * 2**20),
        cost_estimate=pl.CostEstimate(flops=2**16, bytes_accessed=2**20, transcendentals=0),
        name="finish",
    )(mine, other)


def f32(array):
    return array.astype(jnp.float32)


def narrow(*arrays):
    total = f32(arrays[0])
    for array in arrays[1:]:
        total = total + f32(array)
    return total.astype(jnp.bfloat16)


def sum_four(array, axis, bits):
    sent = lax.optimization_barrier(array.astype(jnp.bfloat16))
    one, two = bits
    near, far, both = (lax.ppermute(sent, axis, xor_perm(at)) for at in (one, two, one ^ two))
    return (f32(sent) + f32(near)) + (f32(far) + f32(both))


def pack(array):
    main, row = array[:, :-LANES], array[:16, -LANES:]
    high = lax.reduce_precision(row, 8, 7)
    return jnp.concatenate([main, jnp.concatenate([high, row - high], axis=0)], axis=1)


def unpack(array):
    main, row = array[:, :-LANES], array[:, -LANES:]
    row = row[:16] + row[16:]
    row = jnp.concatenate([row, jnp.zeros_like(row)], axis=0)
    return jnp.concatenate([main, row], axis=1)


def together(*arrays):
    return lax.optimization_barrier(arrays)


def per_device(
    stored_layer_input,
    saved_up_output,
    hidden_gradient,
    frozen_gate_weight,
    lowrank_down,
    lowrank_up,
    magnitude,
):
    own = stored_layer_input
    tokens, height = own.shape
    width = frozen_gate_weight.shape[1]
    low = lowrank_up.shape[0]
    factor = 1.0 / math.sqrt(tokens * lax.axis_size("dp"))
    core = lax.axis_index("dp") % 2
    rank = jnp.stack([lax.axis_index("tensor"), 1 - 2 * core, core]).astype(jnp.int32)
    rank, own = together(rank, own)

    operands = (frozen_gate_weight, jnp.transpose(lowrank_down), lowrank_up)
    head = merge(0, 1, operands, ())

    got = {(0, 0): own}
    token = own[:16, :128]

    def arrive(move, source, target, *more, after=None):
        nonlocal token
        block = got[source]
        if after is not None:
            block, _ = together(block, got[after])
        token, got[target], *more = together(token, move(block), *more)
        return more

    got[0, -1], got[0, 1], got[1, 0], *head = together(
        up_ring(own), down_ring(own), across(own), *head
    )
    merged, square = merge(1, 7, operands, head)
    merged, square = arrive(up_ring, (0, -1), (0, -2), merged, square)
    arrive(across, (0, 1), (1, 1))
    arrive(down_ring, (0, 1), (0, 2))
    total = gate_part(GATE_FIRST, rank, [got[offset] for offset in GATE_FIRST], merged)
    (total,) = arrive(up_ring, (0, -2), (0, -3), total)
    arrive(across, (0, -2), (1, -2))
    arrive(down_ring, (1, 1), (1, 2), after=(0, -2))
    arrive(up_ring, (0, -3), (0, 4))
    arrive(across, (0, -1), (1, -1), after=(0, -3))
    arrive(down_ring, (0, 2), (0, 3), after=(0, -3))
    total = gate_part(
        GATE_SECOND, rank, [got[offset] for offset in GATE_SECOND], merged, (total,)
    )
    (total,) = arrive(up_ring, (1, -2), (1, -3), total, after=(0, -3))
    arrive(down_ring, (1, 2), (1, 3), after=(0, -3))
    total = gate_part(GATE_THIRD, rank, [got[offset] for offset in GATE_THIRD], merged, (total,))
    arrive(across, (0, 4), (1, 4))
    *late, total = together(*[got[offset] for offset in LATE], total)

    up_output_gradient, scaled, both, latent, magnitude_piece, *first = gate_late(
        factor,
        rank,
        late,
        merged,
        total,
        square,
        magnitude.reshape(1, width),
        hidden_gradient,
        saved_up_output,
        lowrank_up,
    )
    lower, upper, far = down_ring(first[0]), up_ring(first[1]), across(first[2])
    up_piece, *others = rest(
        factor, rank, merged, scaled, latent, both, [got[offset] for offset in REST_OUT]
    )
    far, lower, up_piece, *others = together(far, lower, up_piece, *others)
    sums = {offset: [block] for offset, block in zip(REST_OUT, others)}
    sums[0, 4].append(far)
    sums[1, -2].append(lower)

    def land(target, block):
        nonlocal up_piece
        up_piece, block = together(up_piece, block)
        sums[target].append(block)

    def send(move, source, target):
        land(target, move(narrow(*sums[source]) if len(sums[source]) > 1 else sums[source][0]))

    land((1, 2), upper)
    send(down_ring, (0, 4), (0, -3))
    send(up_ring, (1, 2), (1, 1))
    send(across, (1, -2), (0, -2))
    send(up_ring, (0, 3), (0, 2))
    send(down_ring, (0, -3), (0, -2))
    send(across, (1, 1), (0, 1))
    send(across, (1, -1), (0, -1))
    send(up_ring, (0, 2), (0, 1))
    send(down_ring, (0, -2), (0, -1))
    send(across, (1, 0), (0, 0))
    send(up_ring, (0, 1), (0, 0))
    send(down_ring, (0, -1), (0, 0))
    last = together(*sums[0, 0])
    layer_input_gradient = narrow(*[one[:tokens] for one in last])

    kept, sent = payload(
        factor, tokens, rank, up_piece, magnitude_piece, last
    )
    pieces = kept + lax.ppermute(sent, "dp", xor_perm(1))
    pieces = unpack(sum_four(pack(pieces), "dp", (2, 4)))
    sent = lax.optimization_barrier(pack(pieces).astype(jnp.bfloat16))
    pieces = unpack(f32(sent) + f32(lax.ppermute(sent, "dp", xor_perm(8))))
    other = lax.ppermute(pieces[:, :-LANES], "dp", xor_perm(1))
    lowrank_up_gradient, down_gradient, magnitude_gradient = finish(rank, pieces, other, width)
    return (
        layer_input_gradient,
        up_output_gradient,
        jnp.transpose(down_gradient),
        lowrank_up_gradient,
        magnitude_gradient,
    )


def solution(mesh):
    return jax.shard_map(
        per_device,
        mesh=mesh,
        in_specs=(
            P("dp", "tensor"),
            P("dp", "tensor"),
            P("dp", "tensor"),
            P(None, "tensor"),
            P(),
            P(None, "tensor"),
            P("tensor"),
        ),
        out_specs=(
            P("dp", "tensor"),
            P("dp", "tensor"),
            P("tensor", None),
            P(None, "tensor"),
            P("tensor"),
        ),
        check_vma=False,
    )
```
